256 devices in a mesh: row: 16 (over x, z_lo), col: 16 (over y, z_hi, core).
Axes of the slice: x: 4, y: 4, z: 8 (z_hi: 2, z_lo: 4; z = z_hi * 4 + z_lo), core: 2. Of those that a mesh axis runs over, the one named last changes fastest.
Arguments:
- homolog_tensor: bfloat16 [512, 256, 256], P('row', 'col'), may hold values from -6 to 6
- pairwise_tensor: bfloat16 [256, 256, 128], P('row', 'col'), may hold values from -6 to 6
- genuine_amino_flags: int32 [256], replicated, may hold values 0 or 1
- polymer_identity: int32 [256], replicated, may hold values from 0 to 3, never falling along the last dimension, each value on 1 to 128 neighbouring positions
- asking_weights: bfloat16 [256, 256], replicated, may hold values from -0.375 to 0.375
- attend_sigmoid_weights: bfloat16 [256, 256], replicated, may hold values from -0.375 to 0.375
- lookup_content_weights: bfloat16 [256, 512], replicated, may hold values from -0.375 to 0.375
- attend_final_weights: bfloat16 [256, 256], replicated, may hold values from -0.375 to 0.375
- pairwise_logit_weights: bfloat16 [128, 8], replicated, may hold values from -20 to 20
- crosspolymer_offset: float32 [8], replicated, may hold values from -2 to 2
- outgoing_link_weights: bfloat16 [128, 256], replicated, may hold values from -0.5 to 0.5
- incoming_link_weights: bfloat16 [128, 256], replicated, may hold values from -0.5 to 0.5
- trimult_sigmoid_weights: bfloat16 [128, 128], replicated, may hold values from -0.5 to 0.5
- trimult_final_weights: bfloat16 [128, 128], replicated, may hold values from -0.5 to 0.5
Outputs:
- attended_homologs: bfloat16 [512, 256, 256], P('row', 'col')
- pair_output: bfloat16 [256, 256, 128], P('row', 'col')
The draws below stay inside these ranges and needn't reach their ends.
Inputs may be any that keep to these rules, and one draw needn't show every extreme that they name: `polymer_identity`: chain ids never fall along the residues; each chain has 1 to 128 residues and one has exactly that many.
All inputs are finite; a program needn't handle non-finite values.
Results may differ from the reference program's by a relative error of at most 0.0035.
The reference program's roundings to bfloat16 on the way count: a program that leaves them out, or rounds other values in their place, can miss the bound.
Values may be sent and summed in bfloat16 or wider, within the bound.
No kernel may reach another device: no remote copies, remote signals or barrier semaphores. Data moves between devices by JAX's collectives and lax.ppermute only.
A program may use at most 64 MiB of HBM per device.

```python
import math
import jax
import jax.numpy as jnp
import numpy as np
from jax import lax

FEATURE_DEPTH = 256
CZ = 128
H = 8
DH = 32
AMINO_TOTAL = 256
HOMOLOG_TOTAL = 512
ALL_HEADS_SPAN = 256


def draw_pairwise_logit_weights(key, part):
    key = jax.random.fold_in(key, 11)
    base_draw = jnp.clip(jax.random.normal(key, (CZ, H), jnp.float32), -5.0, 5.0)
    return (base_draw * 0.12).astype(jnp.bfloat16)


def place_ends(array, rng, least, top_value):
    index_at = [jax.random.randint(jax.random.fold_in(rng, axis), (), 0, length) for axis, length in enumerate(array.shape)]
    main_axis = array.shape.index(max(array.shape))
    beside = index_at[:main_axis] + [(index_at[main_axis] + 1) % array.shape[main_axis]] + index_at[main_axis + 1:]
    return array.at[tuple(index_at)].set(least).at[tuple(beside)].set(top_value)


def shard_levels(key, dims, shards, least, top_value):
    def one(axis_at, parts):
        heights = jax.random.uniform(jax.random.fold_in(jax.random.fold_in(key, 6), axis_at), (parts,), jnp.float32, least / len(shards), top_value / len(shards))
        return jnp.repeat(jnp.exp(heights), dims[axis_at] // parts).reshape((-1,) + (1,) * (len(dims) - axis_at - 1))

    factor_of = one(*shards[0])
    for cut in shards[1:]:
        factor_of = factor_of * one(*cut)
    return factor_of


def length_profile(amount, total, most, lean):
    portions = [(1 << 20) // math.isqrt(grade ** lean) + 1 for grade in range(2, amount + 1)]
    rest, given = total - most - (amount - 1), [1] * (amount - 1)
    while rest > 0:
        movable = [i for i in range(amount - 1) if given[i] < most]
        whole, left = sum([portions[i] for i in movable]), rest
        for i in movable:
            addition = min(most - given[i], max(1, left * portions[i] // whole), rest)
            given[i] = given[i] + addition
            rest = rest - addition
    return np.array([most] + given)


def uneven_parts(key, amount, total, bound, slope):
    if amount == 2:
        one = jax.random.randint(key, (), max(1, total - bound), min(bound, total - 1) + 1)
        return jnp.stack([one, total - one])
    tallies = jnp.asarray(length_profile(amount, total, bound, slope), jnp.int32)
    twos = (amount - 1) // 2
    giver, taker = tallies[1:1 + 2 * twos:2], tallies[2:2 + 2 * twos:2]
    room = jnp.minimum(giver - 1, bound - taker)
    passed = jax.random.randint(jax.random.fold_in(key, 1), (twos,), 0, 1 << 20) % (room + 1)
    tallies = tallies.at[1:1 + 2 * twos:2].set(giver - passed).at[2:2 + 2 * twos:2].set(taker + passed)
    return tallies[jax.random.permutation(jax.random.fold_in(key, 2), amount)]


def scatter_about(stream_key, dims, scale, reach, cuts=(), kind=jnp.bfloat16):
    result = jax.random.normal(stream_key, dims, jnp.float32) * scale
    if len(cuts) > 0:
        result = shard_levels(stream_key, dims, cuts, -0.22, 0.18) * result
    return jnp.clip(result, min=-reach, max=reach).astype(kind)


def setup_inputs(seed: int = 0) -> dict:
    key_of = jax.random.split(jax.random.key(seed), 15)
    return {
        "homolog_tensor": scatter_about(key_of[0], (HOMOLOG_TOTAL, AMINO_TOTAL, FEATURE_DEPTH), 1.0, 6.0, ((0, 16), (1, 16))),
        "pairwise_tensor": scatter_about(key_of[1], (AMINO_TOTAL, AMINO_TOTAL, CZ), 1.0, 6.0, ((0, 16), (1, 16))),
        "genuine_amino_flags": place_ends((jax.random.randint(key_of[2], (AMINO_TOTAL,), 0, 8) < 7).astype(jnp.int32), jax.random.fold_in(key_of[2], 1), 0, 1),
        "polymer_identity": jnp.searchsorted(jnp.cumsum(uneven_parts(key_of[3], 4, AMINO_TOTAL, AMINO_TOTAL // 2, 0)), jnp.arange(AMINO_TOTAL), side="right").astype(jnp.int32),
        "asking_weights": scatter_about(key_of[4], (FEATURE_DEPTH, ALL_HEADS_SPAN), FEATURE_DEPTH ** -0.5, 0.375),
        "attend_sigmoid_weights": scatter_about(key_of[5], (FEATURE_DEPTH, ALL_HEADS_SPAN), FEATURE_DEPTH ** -0.5, 0.375),
        "lookup_content_weights": scatter_about(key_of[6], (FEATURE_DEPTH, 2 * ALL_HEADS_SPAN), FEATURE_DEPTH ** -0.5, 0.375),
        "attend_final_weights": scatter_about(key_of[7], (ALL_HEADS_SPAN, FEATURE_DEPTH), ALL_HEADS_SPAN ** -0.5, 0.375),
        "pairwise_logit_weights": draw_pairwise_logit_weights(jax.random.fold_in(key_of[14], 71), 0),
        "crosspolymer_offset": jnp.clip(jax.random.uniform(key_of[9], (H,), jnp.float32, -2.0, 2.0), -2.0, 2.0),
        "outgoing_link_weights": scatter_about(key_of[10], (CZ, 2 * CZ), CZ ** -0.5, 0.5),
        "incoming_link_weights": scatter_about(key_of[11], (CZ, 2 * CZ), CZ ** -0.5, 0.5),
        "trimult_sigmoid_weights": scatter_about(key_of[12], (CZ, CZ), CZ ** -0.5, 0.5),
        "trimult_final_weights": scatter_about(key_of[13], (CZ, CZ), CZ ** -0.5, 0.5),
    }


def standardize_features(tensor):
    tensor = tensor.astype(jnp.float32)
    center = tensor - lax.optimization_barrier(jnp.mean(tensor, axis=-1, keepdims=True))
    spread = lax.optimization_barrier(jnp.mean(center * center, axis=-1, keepdims=True))
    return center * lax.rsqrt(spread + 1e-05)

def reference(homolog_tensor, pairwise_tensor, genuine_amino_flags, polymer_identity, asking_weights, attend_sigmoid_weights, lookup_content_weights, attend_final_weights, pairwise_logit_weights, crosspolymer_offset, outgoing_link_weights, incoming_link_weights, trimult_sigmoid_weights, trimult_final_weights):
    standardized_homologs = standardize_features(homolog_tensor).astype(jnp.bfloat16)
    pair_norm = standardize_features(pairwise_tensor).astype(jnp.bfloat16)
    pair_bias = jnp.einsum('ijc,ch->hij', pair_norm.astype(jnp.float32), pairwise_logit_weights.astype(jnp.float32)).astype(jnp.bfloat16)
    cross_chain = (polymer_identity[:, None] != polymer_identity[None, :]).astype(jnp.float32)
    extra_bias = pair_bias.astype(jnp.float32) + crosspolymer_offset[:, None, None] * cross_chain[None]
    keep_keys = (genuine_amino_flags > 0)[None, None, :]

    def single_homolog(split_parts):
        raw_row, norm_row = split_parts
        queries = (jnp.dot(norm_row, asking_weights, preferred_element_type=jnp.float32) * DH ** (-0.5)).astype(jnp.bfloat16)
        key_value = jnp.dot(norm_row, lookup_content_weights, preferred_element_type=jnp.float32).astype(jnp.bfloat16)
        gate_activation = jax.nn.sigmoid(jnp.dot(norm_row, attend_sigmoid_weights, preferred_element_type=jnp.float32))
        q_heads = queries.reshape(AMINO_TOTAL, H, DH).astype(jnp.float32)
        k_heads = key_value[:, :H * DH].reshape(AMINO_TOTAL, H, DH).astype(jnp.float32)
        v_heads = key_value[:, H * DH:].reshape(AMINO_TOTAL, H, DH).astype(jnp.float32)
        scores = jnp.einsum('qhd,khd->hqk', q_heads, k_heads) + extra_bias
        scores = jnp.where(keep_keys, scores, -1000000000.0)
        peak_now = lax.optimization_barrier(jnp.max(scores, axis=-1, keepdims=True))
        exp_scores = jnp.exp(scores - peak_now)
        total_now = lax.optimization_barrier(jnp.sum(exp_scores, axis=-1))
        probs = lax.optimization_barrier(exp_scores.astype(jnp.bfloat16)).astype(jnp.float32)
        attended = jnp.einsum('hqk,khd->qhd', probs, v_heads) / jnp.transpose(total_now)[:, :, None]
        gated_output = (gate_activation * attended.reshape(AMINO_TOTAL, H * DH)).astype(jnp.bfloat16)
        return (raw_row.astype(jnp.float32) + jnp.dot(gated_output, attend_final_weights, preferred_element_type=jnp.float32)).astype(jnp.bfloat16)
    attended_homologs = lax.map(single_homolog, (homolog_tensor, standardized_homologs))
    mask_rows = genuine_amino_flags.astype(jnp.float32)[:, None, None]
    left_proj = jnp.dot(pair_norm, outgoing_link_weights, preferred_element_type=jnp.float32)
    right_proj = jnp.dot(pair_norm, incoming_link_weights, preferred_element_type=jnp.float32)
    left_tri = (mask_rows * jax.nn.sigmoid(left_proj[..., :CZ]) * left_proj[..., CZ:]).astype(jnp.bfloat16)
    right_tri = (mask_rows * jax.nn.sigmoid(right_proj[..., :CZ]) * right_proj[..., CZ:]).astype(jnp.bfloat16)
    product = jnp.einsum('kic,kjc->ijc', left_tri.astype(jnp.float32), right_tri.astype(jnp.float32))
    product_norm = standardize_features(product).astype(jnp.bfloat16)
    tri_gate = jax.nn.sigmoid(jnp.dot(pair_norm, trimult_sigmoid_weights, preferred_element_type=jnp.float32))
    update = jnp.dot(product_norm, trimult_final_weights, preferred_element_type=jnp.float32)
    pair_output = (pairwise_tensor.astype(jnp.float32) + tri_gate * update).astype(jnp.bfloat16)
    return (attended_homologs, pair_output)
```

```python
import jax
import jax.numpy as jnp
from jax import lax
from jax.sharding import PartitionSpec as P

AXES = ("row", "col")
F32 = jnp.float32
BF16 = jnp.bfloat16


def standardize(tensor):
    tensor = tensor.astype(F32)
    center = tensor - jnp.mean(tensor, axis=-1, keepdims=True)
    spread = jnp.mean(center * center, axis=-1, keepdims=True)
    return center * lax.rsqrt(spread + 1e-05)


def dot(a, b):
    return jnp.dot(a, b, preferred_element_type=F32)


def pre(homolog, pair, row_flags, w_q, w_kv, w_bias, w_out, w_in):
    seqs, res, depth = homolog.shape
    heads = w_bias.shape[1]
    width = w_q.shape[1]
    dh = width // heads
    cz = pair.shape[-1]
    msa_norm = standardize(homolog).astype(BF16)
    pair_norm = standardize(pair).astype(BF16)
    queries = (dot(msa_norm, w_q) * dh**-0.5).astype(BF16)
    key_value = dot(msa_norm, w_kv).astype(BF16)
    qkv = jnp.concatenate(
        [a.reshape(seqs, res, heads, dh) for a in (queries, key_value[..., :width], key_value[..., width:])],
        axis=-1,
    )
    qkv = jnp.transpose(qkv, (2, 0, 1, 3)).reshape(heads * seqs, res, 3 * dh)
    bias = jnp.transpose(dot(pair_norm, w_bias).astype(BF16), (2, 0, 1))
    bias = jnp.broadcast_to(bias[:, None], (heads, seqs, res, res)).reshape(heads * seqs, res, res)

    def edges(weight):
        projected = dot(pair_norm, weight)
        edge = row_flags.astype(F32)[:, None, None] * jax.nn.sigmoid(projected[..., :cz]) * projected[..., cz:]
        edge = edge.astype(BF16).reshape(2, res // 2, res, cz)
        return jnp.transpose(edge, (0, 3, 1, 2)).reshape(2 * cz, res // 2, res)

    tri = jnp.concatenate([edges(w_out), edges(w_in)], axis=1)
    return jnp.concatenate([qkv, bias, tri], axis=-1), msa_norm, pair_norm


def mid(received, flags, chain, offset):
    n = 16
    x = received.reshape(n, n * n, 128)
    q, k, v = x[..., :32], x[..., 32:64], x[..., 64:96]
    tiles = received.reshape(n, n, 16, 128)
    bias = jnp.transpose(tiles[..., 96:112], (0, 2, 1, 3)).reshape(256, 256)
    tri = tiles[..., 112:]
    left = jnp.transpose(tri[:, :, :8], (0, 2, 1, 3)).reshape(128, 256)
    right = jnp.transpose(tri[:, :, 8:], (0, 2, 1, 3)).reshape(128, 256)
    cross = (chain[:, None] != chain[None, :]).astype(F32)
    extra = bias.astype(F32) + offset * cross
    scores = jnp.einsum("sid,sjd->sij", q, k, preferred_element_type=F32) + extra
    scores = jnp.where(flags > 0, scores, -1000000000.0)
    exp_scores = jnp.exp(scores - jnp.max(scores, axis=-1, keepdims=True))
    total = jnp.sum(exp_scores, axis=-1)
    attended = jnp.einsum("sij,sjd->sid", exp_scores.astype(BF16), v, preferred_element_type=F32)
    attended = (attended / total[..., None]).astype(BF16)
    product = lax.dot_general(left, right, (((0,), (0,)), ((), ())), preferred_element_type=F32)
    high = product.astype(BF16)
    rest = (product - high.astype(F32)).astype(BF16)

    def tiled(a):
        return jnp.transpose(a.reshape(n, 16, n, 16), (0, 2, 1, 3)).reshape(256, 16, 16)

    chunk = jnp.concatenate([attended.reshape(256, 16, 32), tiled(high), tiled(rest)], axis=-1)
    return jnp.concatenate([chunk[:, :8], chunk[:, 8:]], axis=-1)


def post(received, homolog, pair, msa_norm, pair_norm, w_gate, w_final, w_tri_gate, w_tri_final):
    seqs, res, depth = homolog.shape
    chunk = jnp.concatenate([received[..., :64], received[..., 64:]], axis=1)
    attended = chunk[..., :32].reshape(8, seqs, res, 32)
    attended = jnp.transpose(attended, (1, 2, 0, 3)).reshape(seqs, res, 256)
    gated = (jax.nn.sigmoid(dot(msa_norm, w_gate)) * attended.astype(F32)).astype(BF16)
    out = (homolog.astype(F32) + dot(gated, w_final)).astype(BF16)
    product = chunk[..., 32:48].astype(F32) + chunk[..., 48:64].astype(F32)
    product = jnp.transpose(product[:128] + product[128:], (1, 2, 0))
    product_norm = standardize(product).astype(BF16)
    update = jax.nn.sigmoid(dot(pair_norm, w_tri_gate)) * dot(product_norm, w_tri_final)
    return out, (pair.astype(F32) + update).astype(BF16)


def exchange(chunks):
    return lax.all_to_all(chunks, AXES, split_axis=0, concat_axis=0, tiled=True)


def local(
    homolog_tensor,
    pairwise_tensor,
    genuine_amino_flags,
    polymer_identity,
    asking_weights,
    attend_sigmoid_weights,
    lookup_content_weights,
    attend_final_weights,
    pairwise_logit_weights,
    crosspolymer_offset,
    outgoing_link_weights,
    incoming_link_weights,
    trimult_sigmoid_weights,
    trimult_final_weights,
):
    row = lax.axis_index("row")
    row_flags = lax.dynamic_slice_in_dim(genuine_amino_flags, row * 16, 16, 0)
    send, msa_norm, pair_norm = pre(
        homolog_tensor,
        pairwise_tensor,
        row_flags,
        asking_weights,
        lookup_content_weights,
        pairwise_logit_weights,
        outgoing_link_weights,
        incoming_link_weights,
    )
    back = mid(exchange(send), genuine_amino_flags, polymer_identity, crosspolymer_offset[row // 2])
    return post(
        exchange(back),
        homolog_tensor,
        pairwise_tensor,
        msa_norm,
        pair_norm,
        attend_sigmoid_weights,
        attend_final_weights,
        trimult_sigmoid_weights,
        trimult_final_weights,
    )


def solution(mesh):
    block = P("row", "col", None)
    in_specs = (block, block) + (P(),) * 12
    return jax.shard_map(local, mesh=mesh, in_specs=in_specs, out_specs=(block, block), check_vma=False)
```

```python
import jax
import jax.numpy as jnp
from jax import lax
from jax.experimental import pallas as pl
from jax.experimental.pallas import tpu as pltpu
from jax.sharding import PartitionSpec as P

AXES = ("row", "col")
F32 = jnp.float32
BF16 = jnp.bfloat16
N = 16
HEADS = 8
DH = 32
LANES = 128
VMEM = pl.BlockSpec(memory_space=pltpu.VMEM)
SMEM = pl.BlockSpec(memory_space=pltpu.SMEM)
NT = (((1,), (1,)), ((), ()))
TN = (((0,), (0,)), ((), ()))


def standardize(tensor):
    tensor = tensor.astype(F32)
    center = tensor - jnp.mean(tensor, axis=-1, keepdims=True)
    spread = jnp.mean(center * center, axis=-1, keepdims=True)
    return center * lax.rsqrt(spread + 1e-05)


def dot(a, b, dims=(((1,), (0,)), ((), ()))):
    return lax.dot_general(a, b, dims, preferred_element_type=F32)


def lanes(shape):
    return lax.broadcasted_iota(jnp.int32, shape, len(shape) - 1)


def turn(x, by):
    by = by % LANES
    return x if by == 0 else pltpu.roll(x, by, x.ndim - 1)


def pre_kernel(flags_ref, x_ref, pair_ref, wq_ref, wkv_ref, wb_ref, wo_ref, wi_ref, send_ref, msa_ref, pn_ref, tri_ref, bias_ref):
    row = lax.axis_index("row")
    pair_norm = standardize(pair_ref[...].reshape(N * N, LANES)).astype(BF16)
    pn_ref[...] = pair_norm
    for w_ref, first in ((wo_ref, 0), (wi_ref, 8)):
        projected = dot(pair_norm, w_ref[...])
        edge = (jax.nn.sigmoid(projected[:, :LANES]) * projected[:, LANES:]).T
        for k in range(N):
            half, k8 = k // 8, k % 8
            flag = flags_ref[row * N + k].astype(F32)
            part = turn(edge[:, half * LANES : (half + 1) * LANES], 112 - k8 * 16) * flag
            tri_ref[pl.ds(half * 2048 + first + k8, LANES, stride=16), :] = part
    wb = jnp.concatenate([wb_ref[...].astype(F32), jnp.zeros((LANES, LANES - HEADS), F32)], axis=1).T
    bias = dot(wb[:HEADS].astype(BF16), pair_norm, NT)
    for i in range(N):
        half, i8 = i // 8, i % 8
        bias_ref[pl.ds(i, HEADS, stride=16), :] = turn(bias[:, half * LANES : (half + 1) * LANES], 96 - i8 * 16)

    msa_norm = standardize(x_ref[...].reshape(512, 256)).astype(BF16)
    msa_ref[...] = msa_norm
    lane = lanes((512, LANES))
    for h in range(HEADS):
        cut = slice(h * DH, (h + 1) * DH)
        cut_v = slice(256 + h * DH, 256 + (h + 1) * DH)
        weight = jnp.concatenate([wq_ref[:, cut], wkv_ref[:, cut], wkv_ref[:, cut_v], wq_ref[:, cut]], axis=1)
        y = dot(msa_norm, weight)
        y = jnp.where(lane < DH, y * DH**-0.5, y)
        bias_h = bias_ref[h * 16 : (h + 1) * 16, :]
        bias_h = jnp.broadcast_to(bias_h[None], (32, 16, LANES)).reshape(512, LANES)
        tri = tri_ref[h * 512 : (h + 1) * 512, :]
        out = jnp.where(lane < 96, y, jnp.where(lane < 112, bias_h, tri))
        send_ref[h * 512 : (h + 1) * 512, :] = out.astype(BF16)


def pre(homolog, pair, flags, w_q, w_kv, w_bias, w_out, w_in):
    return pl.pallas_call(
        pre_kernel,
        out_shape=(
            jax.ShapeDtypeStruct((4096, LANES), BF16),
            jax.ShapeDtypeStruct((512, 256), BF16),
            jax.ShapeDtypeStruct((256, LANES), BF16),
        ),
        in_specs=[SMEM] + [VMEM] * 7,
        out_specs=(VMEM, VMEM, VMEM),
        scratch_shapes=[pltpu.VMEM((4096, LANES), F32), pltpu.VMEM((LANES, LANES), F32)],
        compiler_params=pltpu.CompilerParams(vmem_limit_bytes=32 * 2**20),
        name="pre",
    )(flags, homolog, pair, w_q, w_kv, w_bias, w_out, w_in)


def mid_kernel(offset_ref, flags_ref, chain_ref, x_ref, out_ref, ps_ref):
    offset = offset_ref[lax.axis_index("row") // 2]
    wide = (256, LANES)
    slot = lanes(wide) // 16
    bias_cols, tri_cols = [], []
    for half in range(2):
        kept = [None, None]
        for c8 in range(8):
            starts = [(r * N + half * 8 + c8) * 16 for r in range(N)]
            part = jnp.concatenate([x_ref[s : s + 16, :] for s in starts], axis=0).astype(F32)
            part = turn(part, c8 * 16 - 96)
            old = kept[c8 % 2]
            pair_slots = (slot == c8) | (slot == (c8 + 1) % 8)
            kept[c8 % 2] = part if old is None else jnp.where(pair_slots, part, old)
        even = slot % 2 == 0
        bias_cols.append(jnp.where(even, kept[0], kept[1]))
        tri_cols.append(turn(jnp.where(even, kept[1], kept[0]), -16))
    bias = jnp.concatenate(bias_cols, axis=1)
    tri = jnp.concatenate(tri_cols, axis=1).reshape(N, 2, 8, 256)
    left = tri[:, 0].reshape(LANES, 256).T.astype(BF16)
    right = tri[:, 1].reshape(LANES, 256).astype(BF16)
    product = dot(left, right)
    high = product.astype(BF16).astype(F32)
    rest = product - high
    slot8 = lanes((LANES, LANES)) // 16

    for half in range(2):
        cols = slice(half * LANES, (half + 1) * LANES)
        high4 = high[:, cols].reshape(N, 2, 8, LANES)
        rest4 = rest[:, cols].reshape(N, 2, 8, LANES)
        upper = [(high4[:, u].reshape(LANES, LANES), turn(rest4[:, u].reshape(LANES, LANES), 16)) for u in range(2)]
        for parity in range(2):
            ours = slot8 % 2 == parity
            part_a = jnp.where(ours, *upper[0])
            part_b = turn(jnp.where(ours, *upper[1]), 64)
            near = (slot8 >= parity) & (slot8 < parity + 4)
            for merged, firsts in (
                (jnp.where(near, part_a, part_b), (parity, parity + 2)),
                (jnp.where(near, part_b, part_a), (parity + 4, parity + 6)),
            ):
                for c8 in firsts:
                    ps_ref[half * 8 + c8] = turn(merged, 32 - c8 * 16).reshape(N, 8, LANES)

    chain = jnp.broadcast_to(chain_ref[...].astype(F32), (LANES, 256))
    keep = jnp.broadcast_to(flags_ref[...].astype(F32), (LANES, 256))
    chain_t, keep_t = chain.T, keep.T
    bias_t = bias.T
    extra = []
    for half in range(2):
        cols = slice(half * LANES, (half + 1) * LANES)
        cross = jnp.where(chain_t != chain_ref[:, cols].astype(F32), offset, 0.0)
        extra.append(jnp.where(keep_t > 0.0, bias_t[:, cols] + cross, -1000000000.0))
    extra = jnp.concatenate(extra, axis=1)
    keep_k = keep_t[:, :DH].astype(BF16)
    lane3 = lanes((N, 8, LANES))

    for r in range(N):
        x = x_ref[r * 256 : (r + 1) * 256, :]
        scores = dot(x[:, DH : 2 * DH] * keep_k, x[:, :DH], NT) + extra
        exp_scores = jnp.exp(scores - jnp.max(scores, axis=0, keepdims=True))
        total = jnp.sum(exp_scores, axis=0, keepdims=True)
        attended = dot(x[:, 2 * DH : 3 * DH], exp_scores.astype(BF16), TN) / total
        both = jnp.concatenate([attended, attended, attended, attended], axis=0).T.reshape(N, 2, 8, LANES)
        chunk = jnp.where(lane3 < 64, both[:, 0], both[:, 1])
        chunk = jnp.where(lane3 % 64 < DH, chunk, ps_ref[:, r])
        out_ref[r * LANES : (r + 1) * LANES, :] = chunk.reshape(LANES, LANES).astype(BF16)


def mid(received, flags, chain, offset):
    return pl.pallas_call(
        mid_kernel,
        out_shape=jax.ShapeDtypeStruct((2048, LANES), BF16),
        in_specs=[SMEM] + [VMEM] * 3,
        out_specs=VMEM,
        scratch_shapes=[pltpu.VMEM((N, N, 8, LANES), F32)],
        compiler_params=pltpu.CompilerParams(vmem_limit_bytes=32 * 2**20),
        name="mid",
    )(offset, flags.reshape(1, 256), chain.reshape(1, 256), received)


def post_kernel(x_ref, homolog_ref, pair_ref, msa_ref, pn_ref, wg_ref, wf_ref, wtg_ref, wtf_ref, out_ref, pair_out_ref, t_ref):
    x = x_ref[...].astype(F32).reshape(HEADS, 32, 8, LANES)
    group = lanes((32, 8, LANES)) // DH
    attended = []
    for g in range(2):
        parts = [None, None]
        for hh in range(4):
            for u in range(2):
                moved = turn(x[g * 4 + hh], hh * DH - u * 64)
                parts[u] = moved if hh == 0 else jnp.where(group == hh, moved, parts[u])
        attended.append(jnp.stack(parts, axis=1).reshape(512, LANES))
    attended = jnp.concatenate(attended, axis=1)
    gated = (jax.nn.sigmoid(dot(msa_ref[...], wg_ref[...])) * attended).astype(BF16)
    out = homolog_ref[...].reshape(512, 256).astype(F32) + dot(gated, wf_ref[...])
    out_ref[...] = out.astype(BF16).reshape(32, 16, 256)

    t = x.reshape(256, 8, LANES)
    t = t[:LANES] + t[LANES:]
    t = t + turn(t, -16)
    t_ref[...] = t.reshape(1024, LANES)
    upper, lower = [], []
    for i8 in range(8):
        rows = t_ref[pl.ds(i8, LANES, stride=8), :].T
        upper.append(rows[32:48])
        lower.append(rows[96:112])
    product_norm = standardize(jnp.concatenate(upper + lower, axis=0)).astype(BF16)
    update = jax.nn.sigmoid(dot(pn_ref[...], wtg_ref[...])) * dot(product_norm, wtf_ref[...])
    pair_out = pair_ref[...].reshape(N * N, LANES).astype(F32) + update
    pair_out_ref[...] = pair_out.astype(BF16).reshape(N, N, LANES)


def post(received, homolog, pair, msa_norm, pair_norm, w_gate, w_final, w_tri_gate, w_tri_final):
    return pl.pallas_call(
        post_kernel,
        out_shape=(jax.ShapeDtypeStruct(homolog.shape, BF16), jax.ShapeDtypeStruct(pair.shape, BF16)),
        in_specs=[VMEM] * 9,
        out_specs=(VMEM, VMEM),
        scratch_shapes=[pltpu.VMEM((1024, LANES), F32)],
        compiler_params=pltpu.CompilerParams(vmem_limit_bytes=32 * 2**20),
        name="post",
    )(received, homolog, pair, msa_norm, pair_norm, w_gate, w_final, w_tri_gate, w_tri_final)


def exchange(chunks):
    return lax.all_to_all(chunks, AXES, split_axis=0, concat_axis=0, tiled=True)


def local(
    homolog_tensor,
    pairwise_tensor,
    genuine_amino_flags,
    polymer_identity,
    asking_weights,
    attend_sigmoid_weights,
    lookup_content_weights,
    attend_final_weights,
    pairwise_logit_weights,
    crosspolymer_offset,
    outgoing_link_weights,
    incoming_link_weights,
    trimult_sigmoid_weights,
    trimult_final_weights,
):
    send, msa_norm, pair_norm = pre(
        homolog_tensor,
        pairwise_tensor,
        genuine_amino_flags,
        asking_weights,
        lookup_content_weights,
        pairwise_logit_weights,
        outgoing_link_weights,
        incoming_link_weights,
    )
    back = mid(exchange(send), genuine_amino_flags, polymer_identity, crosspolymer_offset)
    return post(
        exchange(back),
        homolog_tensor,
        pairwise_tensor,
        msa_norm,
        pair_norm,
        attend_sigmoid_weights,
        attend_final_weights,
        trimult_sigmoid_weights,
        trimult_final_weights,
    )


def solution(mesh):
    block = P("row", "col", None)
    in_specs = (block, block) + (P(),) * 12
    return jax.shard_map(local, mesh=mesh, in_specs=in_specs, out_specs=(block, block), check_vma=False)
```

```python
import jax
import jax.numpy as jnp
from jax import lax
from jax.experimental import pallas as pl
from jax.experimental.pallas import tpu as pltpu
from jax.sharding import PartitionSpec as P

AXES = ("row", "col")
F32 = jnp.float32
BF16 = jnp.bfloat16
N = 16
HEADS = 8
DH = 32
LANES = 128
VMEM = pl.BlockSpec(memory_space=pltpu.VMEM)
HBM = pl.BlockSpec(memory_space=pltpu.HBM)
NT = (((1,), (1,)), ((), ()))
TN = (((0,), (0,)), ((), ()))


def standardize(tensor):
    tensor = tensor.astype(F32)
    center = tensor - jnp.mean(tensor, axis=-1, keepdims=True)
    spread = jnp.mean(center * center, axis=-1, keepdims=True)
    return center * lax.rsqrt(spread + 1e-05)


def dot(a, b, dims=(((1,), (0,)), ((), ()))):
    return lax.dot_general(a, b, dims, preferred_element_type=F32)


def lanes(shape):
    return lax.broadcasted_iota(jnp.int32, shape, len(shape) - 1)


def turn(x, by):
    by = by % LANES
    return x if by == 0 else pltpu.roll(x, by, x.ndim - 1)


def fetch(pairs, sems):
    copies = [pltpu.make_async_copy(source, target, sems.at[i]) for i, (source, target) in enumerate(pairs)]
    for copy in copies:
        copy.start()
    return copies


def pre_kernel(
    pair_hbm, wo_hbm, wi_hbm, flags_hbm, wb_hbm, x_hbm, wq_hbm, wkv_hbm, offset_hbm, flags2_hbm, chain_hbm,
    send_ref, msa_ref, pn_ref, aux_ref,
    pair_ref, wo_ref, wi_ref, flags_ref, wb_ref, x_ref, wq_ref, wkv_ref, offset_ref, flags2_ref, chain_ref, tri_ref, bias_ref, sems,
):
    row = lax.axis_index("row")
    copies = fetch(
        (
            (pair_hbm, pair_ref),
            (wo_hbm, wo_ref),
            (wi_hbm, wi_ref),
            (flags_hbm, flags_ref),
            (wb_hbm, wb_ref),
            (x_hbm, x_ref),
            (wq_hbm, wq_ref),
            (wkv_hbm, wkv_ref),
            (offset_hbm, offset_ref),
            (flags2_hbm, flags2_ref),
            (chain_hbm, chain_ref),
        ),
        sems,
    )
    for copy in copies[:4]:
        copy.wait()
    pair_norm = standardize(pair_ref[...].reshape(N * N, LANES)).astype(BF16)
    pn_ref[...] = pair_norm
    for w_ref, first in ((wo_ref, 0), (wi_ref, 8)):
        projected = dot(pair_norm, w_ref[...])
        edge = (jax.nn.sigmoid(projected[:, :LANES]) * projected[:, LANES:]).T
        for k in range(N):
            half, k8 = k // 8, k % 8
            flag = flags_ref[row * N + k].astype(F32)
            part = turn(edge[:, half * LANES : (half + 1) * LANES], 112 - k8 * 16) * flag
            tri_ref[pl.ds(half * 2048 + first + k8, LANES, stride=16), :] = part
    copies[4].wait()
    bias = dot(wb_ref[...], pair_norm, NT)
    for i in range(N):
        half, i8 = i // 8, i % 8
        bias_ref[pl.ds(i, HEADS, stride=16), :] = turn(bias[:, half * LANES : (half + 1) * LANES], 96 - i8 * 16)

    for copy in copies[5:]:
        copy.wait()
    msa_norm = standardize(x_ref[...].reshape(512, 256)).astype(BF16)
    msa_ref[...] = msa_norm
    lane = lanes((512, LANES))
    for h in range(0, HEADS, 2):
        parts = []
        for head in (h, h + 1):
            cut = slice(head * DH, (head + 1) * DH)
            cut_v = slice(256 + head * DH, 256 + (head + 1) * DH)
            parts += [wq_ref[:, cut], wkv_ref[:, cut], wkv_ref[:, cut_v], wq_ref[:, cut]]
        both = dot(msa_norm, jnp.concatenate(parts, axis=1))
        for head in (h, h + 1):
            y = both[:, (head - h) * LANES : (head - h + 1) * LANES]
            y = jnp.where(lane < DH, y * DH**-0.5, y)
            bias_h = bias_ref[head * 16 : (head + 1) * 16, :]
            bias_h = jnp.broadcast_to(bias_h[None], (32, 16, LANES)).reshape(512, LANES)
            tri = tri_ref[head * 512 : (head + 1) * 512, :]
            out = jnp.where(lane < 96, y, jnp.where(lane < 112, bias_h, tri))
            send_ref[head * 512 : (head + 1) * 512, :] = out.astype(BF16)
    aux_ref[0:1, :] = flags2_ref[...].astype(F32)
    aux_ref[1:2, :] = chain_ref[...].astype(F32)
    aux_ref[2:3, :] = jnp.full((1, 256), offset_ref[row // 2], F32)


def in_hbm(*arrays):
    return [pltpu.with_memory_space_constraint(a, pltpu.HBM) for a in arrays]


def scratch_like(*arrays):
    return [(pltpu.SMEM if a.ndim == 1 else pltpu.VMEM)(a.shape, a.dtype) for a in arrays]


def pre(homolog, pair, flags, chain, offset, w_q, w_kv, w_bias, w_out, w_in):
    operands = (pair, w_out, w_in, flags, w_bias.T, homolog, w_q, w_kv, offset, flags.reshape(1, 256), chain.reshape(1, 256))
    return pl.pallas_call(
        pre_kernel,
        out_shape=(
            jax.ShapeDtypeStruct((4096, LANES), BF16),
            jax.ShapeDtypeStruct((512, 256), BF16),
            jax.ShapeDtypeStruct((256, LANES), BF16),
            jax.ShapeDtypeStruct((8, 256), F32),
        ),
        in_specs=[HBM] * 11,
        out_specs=(VMEM, VMEM, VMEM, VMEM),
        scratch_shapes=scratch_like(*operands)
        + [pltpu.VMEM((4096, LANES), F32), pltpu.VMEM((LANES, LANES), F32), pltpu.SemaphoreType.DMA((11,))],
        compiler_params=pltpu.CompilerParams(vmem_limit_bytes=32 * 2**20),
        name="pre",
    )(*in_hbm(*operands))


def mid_kernel(aux_ref, x_ref, out_ref, ps_ref):
    wide = (256, LANES)
    slot = lanes(wide) // 16
    bias_cols, tri_cols = [], []
    for half in range(2):
        kept = [None, None]
        for c8 in range(8):
            starts = [(r * N + half * 8 + c8) * 16 for r in range(N)]
            part = jnp.concatenate([x_ref[s : s + 16, :] for s in starts], axis=0).astype(F32)
            part = turn(part, c8 * 16 - 96)
            old = kept[c8 % 2]
            pair_slots = (slot == c8) | (slot == (c8 + 1) % 8)
            kept[c8 % 2] = part if old is None else jnp.where(pair_slots, part, old)
        even = slot % 2 == 0
        bias_cols.append(jnp.where(even, kept[0], kept[1]))
        tri_cols.append(turn(jnp.where(even, kept[1], kept[0]), -16))
    bias = jnp.concatenate(bias_cols, axis=1)
    tri = jnp.concatenate(tri_cols, axis=1).reshape(N, 2, 8, 256)
    left = tri[:, 0].reshape(LANES, 256).T.astype(BF16)
    right = tri[:, 1].reshape(LANES, 256).astype(BF16)
    product = dot(left, right)
    high = product.astype(BF16).astype(F32)
    rest = product - high
    slot8 = lanes((LANES, LANES)) // 16

    for half in range(2):
        cols = slice(half * LANES, (half + 1) * LANES)
        high4 = high[:, cols].reshape(N, 2, 8, LANES)
        rest4 = rest[:, cols].reshape(N, 2, 8, LANES)
        upper = [(high4[:, u].reshape(LANES, LANES), turn(rest4[:, u].reshape(LANES, LANES), 16)) for u in range(2)]
        for parity in range(2):
            ours = slot8 % 2 == parity
            part_a = jnp.where(ours, *upper[0])
            part_b = turn(jnp.where(ours, *upper[1]), 64)
            near = (slot8 >= parity) & (slot8 < parity + 4)
            for merged, firsts in (
                (jnp.where(near, part_a, part_b), (parity, parity + 2)),
                (jnp.where(near, part_b, part_a), (parity + 4, parity + 6)),
            ):
                for c8 in firsts:
                    ps_ref[half * 8 + c8] = turn(merged, 32 - c8 * 16).reshape(N, 8, LANES)

    chain = jnp.broadcast_to(aux_ref[1:2, :], (LANES, 256))
    keep = jnp.broadcast_to(aux_ref[0:1, :], (LANES, 256))
    chain_t, keep_t = chain.T, keep.T
    bias_t = bias.T
    extra = []
    for half in range(2):
        cols = slice(half * LANES, (half + 1) * LANES)
        cross = jnp.where(chain_t != aux_ref[1:2, cols], aux_ref[2:3, cols], 0.0)
        extra.append(jnp.where(keep_t > 0.0, bias_t[:, cols] + cross, -1000000000.0))
    extra = jnp.concatenate(extra, axis=1)
    keep_k = keep_t[:, :DH].astype(BF16)
    lane3 = lanes((N, 8, LANES))

    for r in range(N):
        x = x_ref[r * 256 : (r + 1) * 256, :]
        scores = dot(x[:, DH : 2 * DH] * keep_k, x[:, :DH], NT) + extra
        exp_scores = jnp.exp(scores - jnp.max(scores, axis=0, keepdims=True))
        total = jnp.sum(exp_scores, axis=0, keepdims=True)
        attended = dot(x[:, 2 * DH : 3 * DH], exp_scores.astype(BF16), TN) / total
        both = jnp.concatenate([attended, attended, attended, attended], axis=0).T.reshape(N, 2, 8, LANES)
        chunk = jnp.where(lane3 < 64, both[:, 0], both[:, 1])
        chunk = jnp.where(lane3 % 64 < DH, chunk, ps_ref[:, r])
        out_ref[r * LANES : (r + 1) * LANES, :] = chunk.reshape(LANES, LANES).astype(BF16)


def mid(received, aux):
    return pl.pallas_call(
        mid_kernel,
        out_shape=jax.ShapeDtypeStruct((2048, LANES), BF16),
        in_specs=[VMEM] * 2,
        out_specs=VMEM,
        scratch_shapes=[pltpu.VMEM((N, N, 8, LANES), F32)],
        compiler_params=pltpu.CompilerParams(vmem_limit_bytes=32 * 2**20),
        name="mid",
    )(aux, received)


def post_kernel(x_ref, homolog_ref, pair_ref, msa_ref, pn_ref, wg_ref, wf_ref, wtg_ref, wtf_ref, out_ref, pair_out_ref, t_ref):
    x = x_ref[...].astype(F32).reshape(HEADS, 32, 8, LANES)
    group = lanes((32, 8, LANES)) // DH
    attended = []
    for g in range(2):
        parts = [None, None]
        for hh in range(4):
            for u in range(2):
                moved = turn(x[g * 4 + hh], hh * DH - u * 64)
                parts[u] = moved if hh == 0 else jnp.where(group == hh, moved, parts[u])
        attended.append(jnp.stack(parts, axis=1).reshape(512, LANES))
    attended = jnp.concatenate(attended, axis=1)
    gated = (jax.nn.sigmoid(dot(msa_ref[...], wg_ref[...])) * attended).astype(BF16)
    out = homolog_ref[...].reshape(512, 256).astype(F32) + dot(gated, wf_ref[...])
    out_ref[...] = out.astype(BF16).reshape(32, 16, 256)

    t = x.reshape(256, 8, LANES)
    t = t[:LANES] + t[LANES:]
    t = t + turn(t, -16)
    t_ref[...] = t.reshape(1024, LANES)
    upper, lower = [], []
    for i8 in range(8):
        rows = t_ref[pl.ds(i8, LANES, stride=8), :].T
        upper.append(rows[32:48])
        lower.append(rows[96:112])
    product_norm = standardize(jnp.concatenate(upper + lower, axis=0)).astype(BF16)
    update = jax.nn.sigmoid(dot(pn_ref[...], wtg_ref[...])) * dot(product_norm, wtf_ref[...])
    pair_out = pair_ref[...].reshape(N * N, LANES).astype(F32) + update
    pair_out_ref[...] = pair_out.astype(BF16).reshape(N, N, LANES)


def post(received, homolog, pair, msa_norm, pair_norm, w_gate, w_final, w_tri_gate, w_tri_final):
    return pl.pallas_call(
        post_kernel,
        out_shape=(jax.ShapeDtypeStruct(homolog.shape, BF16), jax.ShapeDtypeStruct(pair.shape, BF16)),
        in_specs=[VMEM] * 9,
        out_specs=(VMEM, VMEM),
        scratch_shapes=[pltpu.VMEM((1024, LANES), F32)],
        compiler_params=pltpu.CompilerParams(vmem_limit_bytes=32 * 2**20),
        name="post",
    )(received, homolog, pair, msa_norm, pair_norm, w_gate, w_final, w_tri_gate, w_tri_final)


def exchange(chunks):
    return lax.all_to_all(chunks, AXES, split_axis=0, concat_axis=0, tiled=True)


def local(
    homolog_tensor,
    pairwise_tensor,
    genuine_amino_flags,
    polymer_identity,
    asking_weights,
    attend_sigmoid_weights,
    lookup_content_weights,
    attend_final_weights,
    pairwise_logit_weights,
    crosspolymer_offset,
    outgoing_link_weights,
    incoming_link_weights,
    trimult_sigmoid_weights,
    trimult_final_weights,
):
    send, msa_norm, pair_norm, aux = pre(
        homolog_tensor,
        pairwise_tensor,
        genuine_amino_flags,
        polymer_identity,
        crosspolymer_offset,
        asking_weights,
        lookup_content_weights,
        pairwise_logit_weights,
        outgoing_link_weights,
        incoming_link_weights,
    )
    back = mid(exchange(send), aux)
    return post(
        exchange(back),
        homolog_tensor,
        pairwise_tensor,
        msa_norm,
        pair_norm,
        attend_sigmoid_weights,
        attend_final_weights,
        trimult_sigmoid_weights,
        trimult_final_weights,
    )


def solution(mesh):
    block = P("row", "col", None)
    in_specs = (block, block) + (P(),) * 12
    return jax.shard_map(local, mesh=mesh, in_specs=in_specs, out_specs=(block, block), check_vma=False)
```

```python
import jax
import jax.numpy as jnp
from jax import lax
from jax.experimental import pallas as pl
from jax.experimental.pallas import tpu as pltpu
from jax.sharding import PartitionSpec as P

AXES = ("row", "col")
F32 = jnp.float32
BF16 = jnp.bfloat16
N = 16
HEADS = 8
DH = 32
LANES = 128
VMEM = pl.BlockSpec(memory_space=pltpu.VMEM)
HBM = pl.BlockSpec(memory_space=pltpu.HBM)
NT = (((1,), (1,)), ((), ()))
TN = (((0,), (0,)), ((), ()))


def standardize(tensor):
    tensor = tensor.astype(F32)
    center = tensor - jnp.mean(tensor, axis=-1, keepdims=True)
    spread = jnp.mean(center * center, axis=-1, keepdims=True)
    return center * lax.rsqrt(spread + 1e-05)


def dot(a, b, dims=(((1,), (0,)), ((), ()))):
    return lax.dot_general(a, b, dims, preferred_element_type=F32)


def lanes(shape):
    return lax.broadcasted_iota(jnp.int32, shape, len(shape) - 1)


def turn(x, by):
    by = by % LANES
    return x if by == 0 else pltpu.roll(x, by, x.ndim - 1)


def fetch(pairs, sems):
    copies = [pltpu.make_async_copy(source, target, sems.at[i]) for i, (source, target) in enumerate(pairs)]
    for copy in copies:
        copy.start()
    return copies


def pre_kernel(
    pair_hbm, wo_hbm, wi_hbm, flags_hbm, wb_hbm, x_hbm, wq_hbm, wkv_hbm, offset_hbm, flags2_hbm, chain_hbm,
    send_ref, msa_ref, pn_ref, aux_ref,
    pair_ref, wo_ref, wi_ref, flags_ref, wb_ref, x_ref, wq_ref, wkv_ref, offset_ref, flags2_ref, chain_ref, tri_ref, bias_ref, sems,
):
    row = lax.axis_index("row")
    copies = fetch(
        (
            (pair_hbm, pair_ref),
            (wo_hbm, wo_ref),
            (wi_hbm, wi_ref),
            (flags_hbm, flags_ref),
            (wb_hbm, wb_ref),
            (x_hbm, x_ref),
            (wq_hbm, wq_ref),
            (wkv_hbm, wkv_ref),
            (offset_hbm, offset_ref),
            (flags2_hbm, flags2_ref),
            (chain_hbm, chain_ref),
        ),
        sems,
    )
    for copy in copies:
        copy.wait()
    msa_norm = standardize(x_ref[...].reshape(512, 256)).astype(BF16)
    msa_ref[...] = msa_norm
    pair_norm = standardize(pair_ref[...].reshape(N * N, LANES)).astype(BF16)
    pn_ref[...] = pair_norm
    for w_ref, first in ((wo_ref, 0), (wi_ref, 8)):
        projected = dot(pair_norm, w_ref[...])
        edge = (jax.nn.sigmoid(projected[:, :LANES]) * projected[:, LANES:]).T
        for k in range(N):
            half, k8 = k // 8, k % 8
            flag = flags_ref[row * N + k].astype(F32)
            part = turn(edge[:, half * LANES : (half + 1) * LANES], 112 - k8 * 16) * flag
            tri_ref[pl.ds(half * 2048 + first + k8, LANES, stride=16), :] = part
    bias = dot(wb_ref[...], pair_norm, NT)
    for i in range(N):
        half, i8 = i // 8, i % 8
        bias_ref[pl.ds(i, HEADS, stride=16), :] = turn(bias[:, half * LANES : (half + 1) * LANES], 96 - i8 * 16)

    lane = lanes((512, LANES))
    for h in range(0, HEADS, 2):
        parts = []
        for head in (h, h + 1):
            cut = slice(head * DH, (head + 1) * DH)
            cut_v = slice(256 + head * DH, 256 + (head + 1) * DH)
            parts += [wq_ref[:, cut], wkv_ref[:, cut], wkv_ref[:, cut_v], wq_ref[:, cut]]
        both = dot(msa_norm, jnp.concatenate(parts, axis=1))
        for head in (h, h + 1):
            y = both[:, (head - h) * LANES : (head - h + 1) * LANES]
            y = jnp.where(lane < DH, y * DH**-0.5, y)
            bias_h = bias_ref[head * 16 : (head + 1) * 16, :]
            bias_h = jnp.broadcast_to(bias_h[None], (32, 16, LANES)).reshape(512, LANES)
            tri = tri_ref[head * 512 : (head + 1) * 512, :]
            out = jnp.where(lane < 96, y, jnp.where(lane < 112, bias_h, tri))
            send_ref[head * 512 : (head + 1) * 512, :] = out.astype(BF16)
    aux_ref[0:1, :] = flags2_ref[...].astype(F32)
    aux_ref[1:2, :] = chain_ref[...].astype(F32)
    aux_ref[2:3, :] = jnp.full((1, 256), offset_ref[row // 2], F32)


def in_hbm(*arrays):
    return [pltpu.with_memory_space_constraint(a, pltpu.HBM) for a in arrays]


def scratch_like(*arrays):
    return [(pltpu.SMEM if a.ndim == 1 else pltpu.VMEM)(a.shape, a.dtype) for a in arrays]


def pre(homolog, pair, flags, chain, offset, w_q, w_kv, w_bias, w_out, w_in):
    operands = (pair, w_out, w_in, flags, w_bias.T, homolog, w_q, w_kv, offset, flags.reshape(1, 256), chain.reshape(1, 256))
    return pl.pallas_call(
        pre_kernel,
        out_shape=(
            jax.ShapeDtypeStruct((4096, LANES), BF16),
            jax.ShapeDtypeStruct((512, 256), BF16),
            jax.ShapeDtypeStruct((256, LANES), BF16),
            jax.ShapeDtypeStruct((8, 256), F32),
        ),
        in_specs=[HBM] * 11,
        out_specs=(VMEM, VMEM, VMEM, VMEM),
        scratch_shapes=scratch_like(*operands)
        + [pltpu.VMEM((4096, LANES), F32), pltpu.VMEM((LANES, LANES), F32), pltpu.SemaphoreType.DMA((11,))],
        compiler_params=pltpu.CompilerParams(vmem_limit_bytes=32 * 2**20),
        name="pre",
    )(*in_hbm(*operands))


def mid_kernel(aux_ref, x_ref, out_ref, ps_ref):
    wide = (256, LANES)
    slot = lanes(wide) // 16
    bias_cols, tri_cols = [], []
    for half in range(2):
        kept = [None, None]
        for c8 in range(8):
            starts = [(r * N + half * 8 + c8) * 16 for r in range(N)]
            part = jnp.concatenate([x_ref[s : s + 16, :] for s in starts], axis=0).astype(F32)
            part = turn(part, c8 * 16 - 96)
            old = kept[c8 % 2]
            pair_slots = (slot == c8) | (slot == (c8 + 1) % 8)
            kept[c8 % 2] = part if old is None else jnp.where(pair_slots, part, old)
        even = slot % 2 == 0
        bias_cols.append(jnp.where(even, kept[0], kept[1]))
        tri_cols.append(turn(jnp.where(even, kept[1], kept[0]), -16))
    bias = jnp.concatenate(bias_cols, axis=1)
    tri = jnp.concatenate(tri_cols, axis=1).reshape(N, 2, 8, 256)
    left = tri[:, 0].reshape(LANES, 256).T.astype(BF16)
    right = tri[:, 1].reshape(LANES, 256).astype(BF16)
    product = dot(left, right)
    high = product.astype(BF16).astype(F32)
    rest = product - high
    slot8 = lanes((LANES, LANES)) // 16

    for half in range(2):
        cols = slice(half * LANES, (half + 1) * LANES)
        high4 = high[:, cols].reshape(N, 2, 8, LANES)
        rest4 = rest[:, cols].reshape(N, 2, 8, LANES)
        upper = [(high4[:, u].reshape(LANES, LANES), turn(rest4[:, u].reshape(LANES, LANES), 16)) for u in range(2)]
        for parity in range(2):
            ours = slot8 % 2 == parity
            part_a = jnp.where(ours, *upper[0])
            part_b = turn(jnp.where(ours, *upper[1]), 64)
            near = (slot8 >= parity) & (slot8 < parity + 4)
            for merged, firsts in (
                (jnp.where(near, part_a, part_b), (parity, parity + 2)),
                (jnp.where(near, part_b, part_a), (parity + 4, parity + 6)),
            ):
                for c8 in firsts:
                    ps_ref[half * 8 + c8] = turn(merged, 32 - c8 * 16).reshape(N, 8, LANES)

    chain = jnp.broadcast_to(aux_ref[1:2, :], (LANES, 256))
    keep = jnp.broadcast_to(aux_ref[0:1, :], (LANES, 256))
    chain_t, keep_t = chain.T, keep.T
    bias_t = bias.T
    extra = []
    for half in range(2):
        cols = slice(half * LANES, (half + 1) * LANES)
        cross = jnp.where(chain_t != aux_ref[1:2, cols], aux_ref[2:3, cols], 0.0)
        extra.append(jnp.where(keep_t > 0.0, bias_t[:, cols] + cross, -1000000000.0))
    extra = jnp.concatenate(extra, axis=1)
    keep_k = keep_t[:, :DH].astype(BF16)
    lane3 = lanes((N, 8, LANES))


    def finish(r, attended):
        both = jnp.concatenate([attended, attended, attended, attended], axis=0).T.reshape(N, 2, 8, LANES)
        chunk = jnp.where(lane3 < 64, both[:, 0], both[:, 1])
        chunk = jnp.where(lane3 % 64 < DH, chunk, ps_ref[:, r])
        out_ref[r * LANES : (r + 1) * LANES, :] = chunk.reshape(LANES, LANES).astype(BF16)

    def scores_of(r):
        x = x_ref[r * 256 : (r + 1) * 256, :]
        return dot(x[:, DH : 2 * DH] * keep_k, x[:, :DH], NT)

    def attend(r, exp_scores, total):
        return dot(x_ref[r * 256 : (r + 1) * 256, :][:, 2 * DH : 3 * DH], exp_scores, TN) / total

    coming = scores_of(0)
    prev = None
    for r in range(N):
        scores = coming + extra
        if r + 1 < N:
            coming = scores_of(r + 1)
        exp_scores = jnp.exp(scores - jnp.max(scores, axis=0, keepdims=True))
        total = jnp.sum(exp_scores, axis=0, keepdims=True)
        if prev is not None:
            finish(r - 1, attend(r - 1, *prev))
        prev = (exp_scores.astype(BF16), total)
    finish(N - 1, attend(N - 1, *prev))


def mid(received, aux):
    return pl.pallas_call(
        mid_kernel,
        out_shape=jax.ShapeDtypeStruct((2048, LANES), BF16),
        in_specs=[VMEM] * 2,
        out_specs=VMEM,
        scratch_shapes=[pltpu.VMEM((N, N, 8, LANES), F32)],
        compiler_params=pltpu.CompilerParams(vmem_limit_bytes=32 * 2**20),
        name="mid",
    )(aux, received)


def post_kernel(x_ref, homolog_ref, pair_ref, msa_ref, pn_ref, wg_ref, wf_ref, wtg_ref, wtf_ref, out_ref, pair_out_ref, t_ref):
    x = x_ref[...].astype(F32).reshape(HEADS, 32, 8, LANES)
    group = lanes((32, 8, LANES)) // DH
    attended = []
    for g in range(2):
        parts = [None, None]
        for hh in range(4):
            for u in range(2):
                moved = turn(x[g * 4 + hh], hh * DH - u * 64)
                parts[u] = moved if hh == 0 else jnp.where(group == hh, moved, parts[u])
        attended.append(jnp.stack(parts, axis=1).reshape(512, LANES))
    attended = jnp.concatenate(attended, axis=1)
    gated = (jax.nn.sigmoid(dot(msa_ref[...], wg_ref[...])) * attended).astype(BF16)
    out = homolog_ref[...].reshape(512, 256).astype(F32) + dot(gated, wf_ref[...])
    out_ref[...] = out.astype(BF16).reshape(32, 16, 256)

    t = x.reshape(256, 8, LANES)
    t = t[:LANES] + t[LANES:]
    t = t + turn(t, -16)
    t_ref[...] = t.reshape(1024, LANES)
    upper, lower = [], []
    for i8 in range(8):
        rows = t_ref[pl.ds(i8, LANES, stride=8), :].T
        upper.append(rows[32:48])
        lower.append(rows[96:112])
    product_norm = standardize(jnp.concatenate(upper + lower, axis=0)).astype(BF16)
    update = jax.nn.sigmoid(dot(pn_ref[...], wtg_ref[...])) * dot(product_norm, wtf_ref[...])
    pair_out = pair_ref[...].reshape(N * N, LANES).astype(F32) + update
    pair_out_ref[...] = pair_out.astype(BF16).reshape(N, N, LANES)


def post(received, homolog, pair, msa_norm, pair_norm, w_gate, w_final, w_tri_gate, w_tri_final):
    return pl.pallas_call(
        post_kernel,
        out_shape=(jax.ShapeDtypeStruct(homolog.shape, BF16), jax.ShapeDtypeStruct(pair.shape, BF16)),
        in_specs=[VMEM] * 9,
        out_specs=(VMEM, VMEM),
        scratch_shapes=[pltpu.VMEM((1024, LANES), F32)],
        compiler_params=pltpu.CompilerParams(vmem_limit_bytes=32 * 2**20),
        name="post",
    )(received, homolog, pair, msa_norm, pair_norm, w_gate, w_final, w_tri_gate, w_tri_final)


def exchange(chunks):
    return lax.all_to_all(chunks, AXES, split_axis=0, concat_axis=0, tiled=True)


def local(
    homolog_tensor,
    pairwise_tensor,
    genuine_amino_flags,
    polymer_identity,
    asking_weights,
    attend_sigmoid_weights,
    lookup_content_weights,
    attend_final_weights,
    pairwise_logit_weights,
    crosspolymer_offset,
    outgoing_link_weights,
    incoming_link_weights,
    trimult_sigmoid_weights,
    trimult_final_weights,
):
    send, msa_norm, pair_norm, aux = pre(
        homolog_tensor,
        pairwise_tensor,
        genuine_amino_flags,
        polymer_identity,
        crosspolymer_offset,
        asking_weights,
        lookup_content_weights,
        pairwise_logit_weights,
        outgoing_link_weights,
        incoming_link_weights,
    )
    back = mid(exchange(send), aux)
    return post(
        exchange(back),
        homolog_tensor,
        pairwise_tensor,
        msa_norm,
        pair_norm,
        attend_sigmoid_weights,
        attend_final_weights,
        trimult_sigmoid_weights,
        trimult_final_weights,
    )


def solution(mesh):
    block = P("row", "col", None)
    in_specs = (block, block) + (P(),) * 12
    return jax.shard_map(local, mesh=mesh, in_specs=in_specs, out_specs=(block, block), check_vma=False)
```

```python
import jax
import jax.numpy as jnp
from jax import lax
from jax.experimental import pallas as pl
from jax.experimental.pallas import tpu as pltpu
from jax.sharding import PartitionSpec as P

AXES = ("row", "col")
F32 = jnp.float32
BF16 = jnp.bfloat16
N = 16
HEADS = 8
DH = 32
LANES = 128
VMEM = pl.BlockSpec(memory_space=pltpu.VMEM)
HBM = pl.BlockSpec(memory_space=pltpu.HBM)
NT = (((1,), (1,)), ((), ()))
TN = (((0,), (0,)), ((), ()))


def standardize(tensor):
    tensor = tensor.astype(F32)
    center = tensor - jnp.mean(tensor, axis=-1, keepdims=True)
    spread = jnp.mean(center * center, axis=-1, keepdims=True)
    return center * lax.rsqrt(spread + 1e-05)


def dot(a, b, dims=(((1,), (0,)), ((), ()))):
    return lax.dot_general(a, b, dims, preferred_element_type=F32)


def lanes(shape):
    return lax.broadcasted_iota(jnp.int32, shape, len(shape) - 1)


def turn(x, by):
    by = by % LANES
    return x if by == 0 else pltpu.roll(x, by, x.ndim - 1)


def fetch(pairs, sems):
    copies = [pltpu.make_async_copy(source, target, sems.at[i]) for i, (source, target) in enumerate(pairs)]
    for copy in copies:
        copy.start()
    return copies


def pre_kernel(
    pair_hbm, wo_hbm, wi_hbm, flags_hbm, wb_hbm, x_hbm, wq_hbm, wkv_hbm, offset_hbm, flags2_hbm, chain_hbm,
    send_ref, msa_ref, pn_ref, aux_ref,
    pair_ref, wo_ref, wi_ref, flags_ref, wb_ref, x_ref, wq_ref, wkv_ref, offset_ref, flags2_ref, chain_ref, tri_ref, bias_ref, sems,
):
    row, col = lax.axis_index("row"), lax.axis_index("col")
    copies = fetch(
        (
            (x_hbm, x_ref),
            (pair_hbm, pair_ref),
            (wo_hbm, wo_ref),
            (wi_hbm, wi_ref),
            (flags_hbm, flags_ref),
            (wb_hbm, wb_ref),
            (wq_hbm, wq_ref),
            (wkv_hbm, wkv_ref),
            (offset_hbm, offset_ref),
            (flags2_hbm, flags2_ref),
            (chain_hbm, chain_ref),
        ),
        sems,
    )
    copies[0].wait()
    msa_norm = standardize(x_ref[...].reshape(512, 256)).astype(BF16)
    msa_ref[...] = msa_norm
    for copy in copies[1:]:
        copy.wait()
    pair_norm = standardize(pair_ref[...].reshape(N * N, LANES)).astype(BF16)
    pn_ref[...] = pair_norm
    for w_ref, first in ((wo_ref, 0), (wi_ref, 8)):
        projected = dot(pair_norm, w_ref[...])
        edge = (jax.nn.sigmoid(projected[:, :LANES]) * projected[:, LANES:]).T
        for k in range(N):
            half, k8 = k // 8, k % 8
            flag = flags_ref[row * N + k].astype(F32)
            part = turn(edge[:, half * LANES : (half + 1) * LANES], 112 - k8 * 16) * flag
            tri_ref[pl.ds(half * 2048 + first + k8, LANES, stride=16), :] = part
    bias = dot(wb_ref[...], pair_norm, NT)
    for i in range(N):
        half, i8 = i // 8, i % 8
        bias_ref[pl.ds(i, HEADS, stride=16), :] = turn(bias[:, half * LANES : (half + 1) * LANES], 96 - i8 * 16)

    lane = lanes((512, LANES))
    tile_row = lax.broadcasted_iota(jnp.int32, (N, LANES), 0)
    keep = jnp.ones((N, LANES), F32)
    for res in range(N):
        keep = jnp.where(tile_row == res, flags_ref[col * N + res].astype(F32), keep)
    tile_lane = lanes((N, LANES))
    factor = jnp.where(tile_lane < DH, DH**-0.5, jnp.where(tile_lane < 2 * DH, keep, 1.0))
    factor = jnp.broadcast_to(factor[None], (32, N, LANES)).reshape(512, LANES)
    for h in range(0, HEADS, 2):
        parts = []
        for head in (h, h + 1):
            cut = slice(head * DH, (head + 1) * DH)
            cut_v = slice(256 + head * DH, 256 + (head + 1) * DH)
            parts += [wq_ref[:, cut], wkv_ref[:, cut], wkv_ref[:, cut_v], wq_ref[:, cut]]
        both = dot(msa_norm, jnp.concatenate(parts, axis=1))
        for head in (h, h + 1):
            y = both[:, (head - h) * LANES : (head - h + 1) * LANES]
            bias_h = bias_ref[head * 16 : (head + 1) * 16, :]
            bias_h = jnp.broadcast_to(bias_h[None], (32, 16, LANES)).reshape(512, LANES)
            tri = tri_ref[head * 512 : (head + 1) * 512, :]
            out = jnp.where(lane < 96, y * factor, jnp.where(lane < 112, bias_h, tri))
            send_ref[head * 512 : (head + 1) * 512, :] = out.astype(BF16)
    aux_ref[0:1, :] = flags2_ref[...].astype(F32)
    aux_ref[1:2, :] = chain_ref[...].astype(F32)
    aux_ref[2:3, :] = jnp.full((1, 256), offset_ref[row // 2], F32)


def in_hbm(*arrays):
    return [pltpu.with_memory_space_constraint(a, pltpu.HBM) for a in arrays]


def scratch_like(*arrays):
    return [(pltpu.SMEM if a.ndim == 1 else pltpu.VMEM)(a.shape, a.dtype) for a in arrays]


def pre(homolog, pair, flags, chain, offset, w_q, w_kv, w_bias, w_out, w_in):
    operands = (pair, w_out, w_in, flags, w_bias.T, homolog, w_q, w_kv, offset, flags.reshape(1, 256), chain.reshape(1, 256))
    return pl.pallas_call(
        pre_kernel,
        out_shape=(
            jax.ShapeDtypeStruct((4096, LANES), BF16),
            jax.ShapeDtypeStruct((512, 256), BF16),
            jax.ShapeDtypeStruct((256, LANES), BF16),
            jax.ShapeDtypeStruct((8, 256), F32),
        ),
        in_specs=[HBM] * 11,
        out_specs=(VMEM, VMEM, VMEM, VMEM),
        scratch_shapes=scratch_like(*operands)
        + [pltpu.VMEM((4096, LANES), F32), pltpu.VMEM((LANES, LANES), F32), pltpu.SemaphoreType.DMA((11,))],
        compiler_params=pltpu.CompilerParams(vmem_limit_bytes=32 * 2**20),
        name="pre",
    )(*in_hbm(*operands))


def mid_kernel(aux_ref, x_ref, out_ref, ps_ref):
    wide = (256, LANES)
    slot = lanes(wide) // 16
    bias_cols, tri_cols = [], []
    for half in range(2):
        kept = [None, None]
        for c8 in range(8):
            starts = [(r * N + half * 8 + c8) * 16 for r in range(N)]
            part = jnp.concatenate([x_ref[s : s + 16, :] for s in starts], axis=0).astype(F32)
            part = turn(part, c8 * 16 - 96)
            old = kept[c8 % 2]
            pair_slots = (slot == c8) | (slot == (c8 + 1) % 8)
            kept[c8 % 2] = part if old is None else jnp.where(pair_slots, part, old)
        even = slot % 2 == 0
        bias_cols.append(jnp.where(even, kept[0], kept[1]))
        tri_cols.append(turn(jnp.where(even, kept[1], kept[0]), -16))
    bias = jnp.concatenate(bias_cols, axis=1)
    tri = jnp.concatenate(tri_cols, axis=1).reshape(N, 2, 8, 256)
    left = tri[:, 0].reshape(LANES, 256).T.astype(BF16)
    right = tri[:, 1].reshape(LANES, 256).astype(BF16)
    product = dot(left, right)
    high = product.astype(BF16).astype(F32)
    rest = product - high
    slot8 = lanes((LANES, LANES)) // 16

    for half in range(2):
        cols = slice(half * LANES, (half + 1) * LANES)
        high4 = high[:, cols].reshape(N, 2, 8, LANES)
        rest4 = rest[:, cols].reshape(N, 2, 8, LANES)
        upper = [(high4[:, u].reshape(LANES, LANES), turn(rest4[:, u].reshape(LANES, LANES), 16)) for u in range(2)]
        for parity in range(2):
            ours = slot8 % 2 == parity
            part_a = jnp.where(ours, *upper[0])
            part_b = turn(jnp.where(ours, *upper[1]), 64)
            near = (slot8 >= parity) & (slot8 < parity + 4)
            for merged, firsts in (
                (jnp.where(near, part_a, part_b), (parity, parity + 2)),
                (jnp.where(near, part_b, part_a), (parity + 4, parity + 6)),
            ):
                for c8 in firsts:
                    ps_ref[half * 8 + c8] = turn(merged, 32 - c8 * 16).reshape(N, 8, LANES)

    chain = jnp.broadcast_to(aux_ref[1:2, :], (LANES, 256))
    keep = jnp.broadcast_to(aux_ref[0:1, :], (LANES, 256))
    chain_t, keep_t = chain.T, keep.T
    bias_t = bias.T
    extra = []
    for half in range(2):
        cols = slice(half * LANES, (half + 1) * LANES)
        cross = jnp.where(chain_t != aux_ref[1:2, cols], aux_ref[2:3, cols], 0.0)
        extra.append(jnp.where(keep_t > 0.0, bias_t[:, cols] + cross, -1000000000.0))
    extra = jnp.concatenate(extra, axis=1)
    lane3 = lanes((N, 8, LANES))


    def finish(r, attended):
        both = jnp.concatenate([attended, attended, attended, attended], axis=0).T.reshape(N, 2, 8, LANES)
        chunk = jnp.where(lane3 < 64, both[:, 0], both[:, 1])
        chunk = jnp.where(lane3 % 64 < DH, chunk, ps_ref[:, r])
        out_ref[r * LANES : (r + 1) * LANES, :] = chunk.reshape(LANES, LANES).astype(BF16)

    def scores_of(r):
        x = x_ref[r * 256 : (r + 1) * 256, :]
        return dot(x[:, DH : 2 * DH], x[:, :DH], NT)

    def attend(r, exp_scores, total):
        return dot(x_ref[r * 256 : (r + 1) * 256, :], exp_scores, TN)[2 * DH : 3 * DH] / total

    coming = scores_of(0)
    prev = None
    for r in range(N):
        scores = coming + extra
        if r + 1 < N:
            coming = scores_of(r + 1)
        exp_scores = jnp.exp(scores - jnp.max(scores, axis=0, keepdims=True))
        total = jnp.sum(exp_scores, axis=0, keepdims=True)
        if prev is not None:
            finish(r - 1, attend(r - 1, *prev))
        prev = (exp_scores.astype(BF16), total)
    finish(N - 1, attend(N - 1, *prev))


def mid(received, aux):
    return pl.pallas_call(
        mid_kernel,
        out_shape=jax.ShapeDtypeStruct((2048, LANES), BF16),
        in_specs=[VMEM] * 2,
        out_specs=VMEM,
        scratch_shapes=[pltpu.VMEM((N, N, 8, LANES), F32)],
        compiler_params=pltpu.CompilerParams(vmem_limit_bytes=32 * 2**20),
        name="mid",
    )(aux, received)


def post_kernel(x_ref, homolog_ref, pair_ref, msa_ref, pn_ref, wg_ref, wf_ref, wtg_ref, wtf_ref, out_ref, pair_out_ref, t_ref):
    x = x_ref[...].astype(F32).reshape(HEADS, 32, 8, LANES)
    group = lanes((32, 8, LANES)) // DH
    attended = []
    for g in range(2):
        parts = [None, None]
        for hh in range(4):
            for u in range(2):
                moved = turn(x[g * 4 + hh], hh * DH - u * 64)
                parts[u] = moved if hh == 0 else jnp.where(group == hh, moved, parts[u])
        attended.append(jnp.stack(parts, axis=1).reshape(512, LANES))
    attended = jnp.concatenate(attended, axis=1)
    gated = (jax.nn.sigmoid(dot(msa_ref[...], wg_ref[...])) * attended).astype(BF16)
    out = homolog_ref[...].reshape(512, 256).astype(F32) + dot(gated, wf_ref[...])
    out_ref[...] = out.astype(BF16).reshape(32, 16, 256)

    t = x.reshape(256, 8, LANES)
    t = t[:LANES] + t[LANES:]
    t = t + turn(t, -16)
    t_ref[...] = t.reshape(1024, LANES)
    upper, lower = [], []
    for i8 in range(8):
        rows = t_ref[pl.ds(i8, LANES, stride=8), :].T
        upper.append(rows[32:48])
        lower.append(rows[96:112])
    product_norm = standardize(jnp.concatenate(upper + lower, axis=0)).astype(BF16)
    update = jax.nn.sigmoid(dot(pn_ref[...], wtg_ref[...])) * dot(product_norm, wtf_ref[...])
    pair_out = pair_ref[...].reshape(N * N, LANES).astype(F32) + update
    pair_out_ref[...] = pair_out.astype(BF16).reshape(N, N, LANES)


def post(received, homolog, pair, msa_norm, pair_norm, w_gate, w_final, w_tri_gate, w_tri_final):
    return pl.pallas_call(
        post_kernel,
        out_shape=(jax.ShapeDtypeStruct(homolog.shape, BF16), jax.ShapeDtypeStruct(pair.shape, BF16)),
        in_specs=[VMEM] * 9,
        out_specs=(VMEM, VMEM),
        scratch_shapes=[pltpu.VMEM((1024, LANES), F32)],
        compiler_params=pltpu.CompilerParams(vmem_limit_bytes=32 * 2**20),
        name="post",
    )(received, homolog, pair, msa_norm, pair_norm, w_gate, w_final, w_tri_gate, w_tri_final)


def exchange(chunks):
    return lax.all_to_all(chunks, AXES, split_axis=0, concat_axis=0, tiled=True)


def local(
    homolog_tensor,
    pairwise_tensor,
    genuine_amino_flags,
    polymer_identity,
    asking_weights,
    attend_sigmoid_weights,
    lookup_content_weights,
    attend_final_weights,
    pairwise_logit_weights,
    crosspolymer_offset,
    outgoing_link_weights,
    incoming_link_weights,
    trimult_sigmoid_weights,
    trimult_final_weights,
):
    send, msa_norm, pair_norm, aux = pre(
        homolog_tensor,
        pairwise_tensor,
        genuine_amino_flags,
        polymer_identity,
        crosspolymer_offset,
        asking_weights,
        lookup_content_weights,
        pairwise_logit_weights,
        outgoing_link_weights,
        incoming_link_weights,
    )
    back = mid(exchange(send), aux)
    return post(
        exchange(back),
        homolog_tensor,
        pairwise_tensor,
        msa_norm,
        pair_norm,
        attend_sigmoid_weights,
        attend_final_weights,
        trimult_sigmoid_weights,
        trimult_final_weights,
    )


def solution(mesh):
    block = P("row", "col", None)
    in_specs = (block, block) + (P(),) * 12
    return jax.shard_map(local, mesh=mesh, in_specs=in_specs, out_specs=(block, block), check_vma=False)
```

```python
import jax
import jax.numpy as jnp
from jax import lax
from jax.experimental import pallas as pl
from jax.experimental.pallas import tpu as pltpu
from jax.sharding import PartitionSpec as P

AXES = ("row", "col")
F32 = jnp.float32
BF16 = jnp.bfloat16
N = 16
HEADS = 8
DH = 32
LANES = 128
VMEM = pl.BlockSpec(memory_space=pltpu.VMEM)
HBM = pl.BlockSpec(memory_space=pltpu.HBM)
NT = (((1,), (1,)), ((), ()))
TN = (((0,), (0,)), ((), ()))


def standardize(tensor):
    tensor = tensor.astype(F32)
    center = tensor - jnp.mean(tensor, axis=-1, keepdims=True)
    spread = jnp.mean(center * center, axis=-1, keepdims=True)
    return center * lax.rsqrt(spread + 1e-05)


def dot(a, b, dims=(((1,), (0,)), ((), ()))):
    return lax.dot_general(a, b, dims, preferred_element_type=F32)


def lanes(shape):
    return lax.broadcasted_iota(jnp.int32, shape, len(shape) - 1)


def turn(x, by):
    by = by % LANES
    return x if by == 0 else pltpu.roll(x, by, x.ndim - 1)


def fetch(pairs, sems):
    copies = [pltpu.make_async_copy(source, target, sems.at[i]) for i, (source, target) in enumerate(pairs)]
    for copy in copies:
        copy.start()
    return copies


def pre_kernel(
    pair_hbm, wo_hbm, wi_hbm, flags_hbm, wb_hbm, x_hbm, wq_hbm, wkv_hbm, offset_hbm, flags2_hbm, chain_hbm,
    send_ref, msa_ref, pn_ref, aux_ref,
    pair_ref, wo_ref, wi_ref, flags_ref, wb_ref, x_ref, wq_ref, wkv_ref, offset_ref, flags2_ref, chain_ref, tri_ref, bias_ref, sems,
):
    row, col = lax.axis_index("row"), lax.axis_index("col")
    copies = fetch(
        (
            (x_hbm, x_ref),
            (pair_hbm, pair_ref),
            (wo_hbm, wo_ref),
            (wi_hbm, wi_ref),
            (flags_hbm, flags_ref),
            (wb_hbm, wb_ref),
            (wq_hbm, wq_ref),
            (wkv_hbm, wkv_ref),
            (offset_hbm, offset_ref),
            (flags2_hbm, flags2_ref),
            (chain_hbm, chain_ref),
        ),
        sems,
    )
    copies[0].wait()
    msa_norm = standardize(x_ref[...].reshape(512, 256)).astype(BF16)
    msa_ref[...] = msa_norm
    for copy in copies[1:]:
        copy.wait()
    pair_norm = standardize(pair_ref[...].reshape(N * N, LANES)).astype(BF16)
    pn_ref[...] = pair_norm
    lane8 = lanes((LANES, LANES))
    sides = []
    for w_ref in (wo_ref, wi_ref):
        projected = dot(pair_norm, w_ref[...])
        sides.append((jax.nn.sigmoid(projected[:, :LANES]) * projected[:, LANES:]).T)
    for k in range(N):
        half, k8 = k // 8, k % 8
        flag = flags_ref[row * N + k].astype(F32)
        left, right = (side[:, half * LANES : (half + 1) * LANES] for side in sides)
        part = jnp.where(lane8 < 112, turn(left, 96 - k8 * 16), turn(right, 112 - k8 * 16)) * flag
        tri_ref[pl.ds(half * 1024 + k8, LANES, stride=8), :] = part
    bias = dot(wb_ref[...], pair_norm, NT)
    for i in range(8):
        part = jnp.where(lane8[:8] < 112, turn(bias[:, :LANES], 96 - i * 16), turn(bias[:, LANES:], 112 - i * 16))
        bias_ref[pl.ds(i, HEADS, stride=8), :] = part

    lane = lanes((512, LANES))
    tile_row = lax.broadcasted_iota(jnp.int32, (N, LANES), 0)
    keep = jnp.ones((N, LANES), F32)
    for res in range(N):
        keep = jnp.where(tile_row == res, flags_ref[col * N + res].astype(F32), keep)
    tile_lane = lanes((N, LANES))
    factor = jnp.where(tile_lane < DH, DH**-0.5, jnp.where(tile_lane < 2 * DH, keep, 1.0))
    factor = jnp.broadcast_to(factor[None], (32, N, LANES)).reshape(512, LANES)
    for h in range(0, HEADS, 2):
        parts = []
        for head in (h, h + 1):
            cut = slice(head * DH, (head + 1) * DH)
            cut_v = slice(256 + head * DH, 256 + (head + 1) * DH)
            parts += [wq_ref[:, cut], wkv_ref[:, cut], wkv_ref[:, cut_v], wq_ref[:, cut]]
        both = dot(msa_norm, jnp.concatenate(parts, axis=1))
        for head in (h, h + 1):
            y = both[:, (head - h) * LANES : (head - h + 1) * LANES]
            tri = tri_ref[head * 256 : (head + 1) * 256, :].reshape(32, 8, LANES)
            bias_h = jnp.broadcast_to(bias_ref[head * 8 : (head + 1) * 8, :][None], (32, 8, LANES))
            tail = jnp.stack([tri, bias_h], axis=1).reshape(512, LANES)
            out = jnp.where(lane < 96, y * factor, tail)
            send_ref[head * 512 : (head + 1) * 512, :] = out.astype(BF16)
    aux_ref[0:1, :] = flags2_ref[...].astype(F32)
    aux_ref[1:2, :] = chain_ref[...].astype(F32)
    aux_ref[2:3, :] = jnp.full((1, 256), offset_ref[row // 2], F32)


def in_hbm(*arrays):
    return [pltpu.with_memory_space_constraint(a, pltpu.HBM) for a in arrays]


def scratch_like(*arrays):
    return [(pltpu.SMEM if a.ndim == 1 else pltpu.VMEM)(a.shape, a.dtype) for a in arrays]


def pre(homolog, pair, flags, chain, offset, w_q, w_kv, w_bias, w_out, w_in):
    operands = (pair, w_out, w_in, flags, w_bias.T, homolog, w_q, w_kv, offset, flags.reshape(1, 256), chain.reshape(1, 256))
    return pl.pallas_call(
        pre_kernel,
        out_shape=(
            jax.ShapeDtypeStruct((4096, LANES), BF16),
            jax.ShapeDtypeStruct((512, 256), BF16),
            jax.ShapeDtypeStruct((256, LANES), BF16),
            jax.ShapeDtypeStruct((8, 256), F32),
        ),
        in_specs=[HBM] * 11,
        out_specs=(VMEM, VMEM, VMEM, VMEM),
        scratch_shapes=scratch_like(*operands)
        + [pltpu.VMEM((2048, LANES), F32), pltpu.VMEM((HEADS * 8, LANES), F32), pltpu.SemaphoreType.DMA((11,))],
        compiler_params=pltpu.CompilerParams(vmem_limit_bytes=32 * 2**20),
        name="pre",
    )(*in_hbm(*operands))


def mid_kernel(aux_ref, x_ref, out_ref, ps_ref, scores_ref):
    wide = (256, LANES)
    slot = lanes(wide) // 16
    def key_query(r):
        x = x_ref[r * 256 : (r + 1) * 256, :]
        return dot(x[:, DH : 2 * DH], x[:, :DH], NT)

    for r in range(N):
        scores_ref[r] = key_query(r)

    firsts, seconds = [], []
    for half in range(2):
        kept = [None, None]
        for c8 in range(8):
            starts = [(r * N + half * 8 + c8) * 16 for r in range(N)]
            part = jnp.concatenate([x_ref[s : s + 16, :] for s in starts], axis=0).astype(F32)
            part = turn(part, c8 * 16 - 96)
            old = kept[c8 % 2]
            pair_slots = (slot == c8) | (slot == (c8 + 1) % 8)
            kept[c8 % 2] = part if old is None else jnp.where(pair_slots, part, old)
        even = slot % 2 == 0
        firsts.append(jnp.where(even, kept[0], kept[1]))
        seconds.append(turn(jnp.where(even, kept[1], kept[0]), -16))
    first = jnp.concatenate(firsts, axis=1).reshape(N, 2, 8, 256)
    second = jnp.concatenate(seconds, axis=1).reshape(N, 2, 8, 256)
    bias = jnp.stack([first[:, 1], second[:, 1]], axis=1).reshape(256, 256)
    left = first[:, 0].reshape(LANES, 256).T.astype(BF16)
    right = second[:, 0].reshape(LANES, 256).astype(BF16)
    product = dot(left, right)
    high = product.astype(BF16).astype(F32)
    rest = product - high
    slot8 = lanes((LANES, LANES)) // 16

    for half in range(2):
        cols = slice(half * LANES, (half + 1) * LANES)
        high4 = high[:, cols].reshape(N, 2, 8, LANES)
        rest4 = rest[:, cols].reshape(N, 2, 8, LANES)
        upper = [(high4[:, u].reshape(LANES, LANES), turn(rest4[:, u].reshape(LANES, LANES), 16)) for u in range(2)]
        for parity in range(2):
            ours = slot8 % 2 == parity
            part_a = jnp.where(ours, *upper[0])
            part_b = turn(jnp.where(ours, *upper[1]), 64)
            near = (slot8 >= parity) & (slot8 < parity + 4)
            for merged, firsts in (
                (jnp.where(near, part_a, part_b), (parity, parity + 2)),
                (jnp.where(near, part_b, part_a), (parity + 4, parity + 6)),
            ):
                for c8 in firsts:
                    ps_ref[half * 8 + c8] = turn(merged, 32 - c8 * 16).reshape(N, 8, LANES)

    chain = jnp.broadcast_to(aux_ref[1:2, :], (LANES, 256))
    keep = jnp.broadcast_to(aux_ref[0:1, :], (LANES, 256))
    chain_t, keep_t = chain.T, keep.T
    bias_t = bias.T
    extra = []
    for half in range(2):
        cols = slice(half * LANES, (half + 1) * LANES)
        cross = jnp.where(chain_t != aux_ref[1:2, cols], aux_ref[2:3, cols], 0.0)
        extra.append(jnp.where(keep_t > 0.0, bias_t[:, cols] + cross, -1000000000.0))
    extra = jnp.concatenate(extra, axis=1)
    lane3 = lanes((N, 8, LANES))


    def finish(r, attended):
        both = jnp.concatenate([attended, attended, attended, attended], axis=0).T.reshape(N, 2, 8, LANES)
        chunk = jnp.where(lane3 < 64, both[:, 0], both[:, 1])
        chunk = jnp.where(lane3 % 64 < DH, chunk, ps_ref[:, r])
        out_ref[r * LANES : (r + 1) * LANES, :] = chunk.reshape(LANES, LANES).astype(BF16)

    def attend(r, exp_scores, total):
        return dot(x_ref[r * 256 : (r + 1) * 256, :], exp_scores, TN)[2 * DH : 3 * DH] / total

    coming = scores_ref[0]
    prev = None
    for r in range(N):
        scores = coming + extra
        if r + 1 < N:
            coming = scores_ref[r + 1]
        exp_scores = jnp.exp(scores - jnp.max(scores, axis=0, keepdims=True))
        total = jnp.sum(exp_scores, axis=0, keepdims=True)
        if prev is not None:
            finish(r - 1, attend(r - 1, *prev))
        prev = (exp_scores.astype(BF16), total)
    finish(N - 1, attend(N - 1, *prev))


def mid(received, aux):
    return pl.pallas_call(
        mid_kernel,
        out_shape=jax.ShapeDtypeStruct((2048, LANES), BF16),
        in_specs=[VMEM] * 2,
        out_specs=VMEM,
        scratch_shapes=[pltpu.VMEM((N, N, 8, LANES), F32), pltpu.VMEM((N, 256, 256), F32)],
        compiler_params=pltpu.CompilerParams(vmem_limit_bytes=32 * 2**20),
        name="mid",
    )(aux, received)


def post_kernel(x_ref, homolog_ref, pair_ref, msa_ref, pn_ref, wg_ref, wf_ref, wtg_ref, wtf_ref, out_ref, pair_out_ref, t_ref):
    x = x_ref[...].astype(F32).reshape(HEADS, 32, 8, LANES)
    group = lanes((32, 8, LANES)) // DH
    attended = []
    for g in range(2):
        parts = [None, None]
        for hh in range(4):
            for u in range(2):
                moved = turn(x[g * 4 + hh], hh * DH - u * 64)
                parts[u] = moved if hh == 0 else jnp.where(group == hh, moved, parts[u])
        attended.append(jnp.stack(parts, axis=1).reshape(512, LANES))
    attended = jnp.concatenate(attended, axis=1)
    gated = (jax.nn.sigmoid(dot(msa_ref[...], wg_ref[...])) * attended).astype(BF16)
    out = homolog_ref[...].reshape(512, 256).astype(F32) + dot(gated, wf_ref[...])
    out_ref[...] = out.astype(BF16).reshape(32, 16, 256)

    t = x.reshape(256, 8, LANES)
    t = t[:LANES] + t[LANES:]
    t = t + turn(t, -16)
    t_ref[...] = t.reshape(1024, LANES)
    upper, lower = [], []
    for i8 in range(8):
        rows = t_ref[pl.ds(i8, LANES, stride=8), :].T
        upper.append(rows[32:48])
        lower.append(rows[96:112])
    product_norm = standardize(jnp.concatenate(upper + lower, axis=0)).astype(BF16)
    update = jax.nn.sigmoid(dot(pn_ref[...], wtg_ref[...])) * dot(product_norm, wtf_ref[...])
    pair_out = pair_ref[...].reshape(N * N, LANES).astype(F32) + update
    pair_out_ref[...] = pair_out.astype(BF16).reshape(N, N, LANES)


def post(received, homolog, pair, msa_norm, pair_norm, w_gate, w_final, w_tri_gate, w_tri_final):
    return pl.pallas_call(
        post_kernel,
        out_shape=(jax.ShapeDtypeStruct(homolog.shape, BF16), jax.ShapeDtypeStruct(pair.shape, BF16)),
        in_specs=[VMEM] * 9,
        out_specs=(VMEM, VMEM),
        scratch_shapes=[pltpu.VMEM((1024, LANES), F32)],
        compiler_params=pltpu.CompilerParams(vmem_limit_bytes=32 * 2**20),
        name="post",
    )(received, homolog, pair, msa_norm, pair_norm, w_gate, w_final, w_tri_gate, w_tri_final)


def exchange(chunks):
    return lax.all_to_all(chunks, AXES, split_axis=0, concat_axis=0, tiled=True)


def local(
    homolog_tensor,
    pairwise_tensor,
    genuine_amino_flags,
    polymer_identity,
    asking_weights,
    attend_sigmoid_weights,
    lookup_content_weights,
    attend_final_weights,
    pairwise_logit_weights,
    crosspolymer_offset,
    outgoing_link_weights,
    incoming_link_weights,
    trimult_sigmoid_weights,
    trimult_final_weights,
):
    send, msa_norm, pair_norm, aux = pre(
        homolog_tensor,
        pairwise_tensor,
        genuine_amino_flags,
        polymer_identity,
        crosspolymer_offset,
        asking_weights,
        lookup_content_weights,
        pairwise_logit_weights,
        outgoing_link_weights,
        incoming_link_weights,
    )
    back = mid(exchange(send), aux)
    return post(
        exchange(back),
        homolog_tensor,
        pairwise_tensor,
        msa_norm,
        pair_norm,
        attend_sigmoid_weights,
        attend_final_weights,
        trimult_sigmoid_weights,
        trimult_final_weights,
    )


def solution(mesh):
    block = P("row", "col", None)
    in_specs = (block, block) + (P(),) * 12
    return jax.shard_map(local, mesh=mesh, in_specs=in_specs, out_specs=(block, block), check_vma=False)
```

```python
import jax
import jax.numpy as jnp
from jax import lax
from jax.experimental import pallas as pl
from jax.experimental.pallas import tpu as pltpu
from jax.sharding import PartitionSpec as P

AXES = ("row", "col")
F32 = jnp.float32
BF16 = jnp.bfloat16
N = 16
HEADS = 8
DH = 32
LANES = 128
VMEM = pl.BlockSpec(memory_space=pltpu.VMEM)
HBM = pl.BlockSpec(memory_space=pltpu.HBM)
NT = (((1,), (1,)), ((), ()))
TN = (((0,), (0,)), ((), ()))


def standardize(tensor):
    tensor = tensor.astype(F32)
    center = tensor - jnp.mean(tensor, axis=-1, keepdims=True)
    spread = jnp.mean(center * center, axis=-1, keepdims=True)
    return center * lax.rsqrt(spread + 1e-05)


def dot(a, b, dims=(((1,), (0,)), ((), ()))):
    return lax.dot_general(a, b, dims, preferred_element_type=F32)


def lanes(shape):
    return lax.broadcasted_iota(jnp.int32, shape, len(shape) - 1)


def turn(x, by):
    by = by % LANES
    return x if by == 0 else pltpu.roll(x, by, x.ndim - 1)


def fetch(pairs, sems):
    copies = [pltpu.make_async_copy(source, target, sems.at[i]) for i, (source, target) in enumerate(pairs)]
    for copy in copies:
        copy.start()
    return copies


def pre_kernel(
    pair_hbm, wo_hbm, wi_hbm, flags_hbm, wb_hbm, x_hbm, wq_hbm, wkv_hbm, offset_hbm, flags2_hbm, chain_hbm,
    send_ref, msa_ref, pn_ref, aux_ref,
    pair_ref, wo_ref, wi_ref, flags_ref, wb_ref, x_ref, wq_ref, wkv_ref, offset_ref, flags2_ref, chain_ref, tri_ref, bias_ref, sems,
):
    row, col = lax.axis_index("row"), lax.axis_index("col")
    copies = fetch(
        (
            (x_hbm, x_ref),
            (pair_hbm, pair_ref),
            (wo_hbm, wo_ref),
            (wi_hbm, wi_ref),
            (flags_hbm, flags_ref),
            (wb_hbm, wb_ref),
            (wq_hbm, wq_ref),
            (wkv_hbm, wkv_ref),
            (offset_hbm, offset_ref),
            (flags2_hbm, flags2_ref),
            (chain_hbm, chain_ref),
        ),
        sems,
    )
    copies[0].wait()
    msa_norm = standardize(x_ref[...].reshape(512, 256)).astype(BF16)
    msa_ref[...] = msa_norm
    for copy in copies[1:]:
        copy.wait()
    pair_norm = standardize(pair_ref[...].reshape(N * N, LANES)).astype(BF16)
    pn_ref[...] = pair_norm
    lane8 = lanes((LANES, LANES))
    sides = []
    for w_ref in (wo_ref, wi_ref):
        projected = dot(pair_norm, w_ref[...])
        sides.append((jax.nn.sigmoid(projected[:, :LANES]) * projected[:, LANES:]).T)
    for k in range(N):
        half, k8 = k // 8, k % 8
        flag = flags_ref[row * N + k].astype(F32)
        left, right = (side[:, half * LANES : (half + 1) * LANES] for side in sides)
        part = jnp.where(lane8 < 112, turn(left, 96 - k8 * 16), turn(right, 112 - k8 * 16)) * flag
        tri_ref[pl.ds(half * 1024 + k8, LANES, stride=8), :] = part
    bias = dot(wb_ref[...], pair_norm, NT)
    for i in range(8):
        part = jnp.where(lane8[:8] < 112, turn(bias[:, :LANES], 96 - i * 16), turn(bias[:, LANES:], 112 - i * 16))
        bias_ref[pl.ds(i, HEADS, stride=8), :] = part

    lane = lanes((512, LANES))
    tile_row = lax.broadcasted_iota(jnp.int32, (N, LANES), 0)
    keep = jnp.ones((N, LANES), F32)
    for res in range(N):
        keep = jnp.where(tile_row == res, flags_ref[col * N + res].astype(F32), keep)
    tile_lane = lanes((N, LANES))
    factor = jnp.where(tile_lane < DH, DH**-0.5, jnp.where(tile_lane < 2 * DH, keep, 1.0))
    factor = jnp.broadcast_to(factor[None], (32, N, LANES)).reshape(512, LANES)
    for h in range(0, HEADS, 2):
        parts = []
        for head in (h, h + 1):
            cut = slice(head * DH, (head + 1) * DH)
            cut_v = slice(256 + head * DH, 256 + (head + 1) * DH)
            parts += [wq_ref[:, cut], wkv_ref[:, cut], wkv_ref[:, cut_v], wq_ref[:, cut]]
        both = dot(msa_norm, jnp.concatenate(parts, axis=1))
        for head in (h, h + 1):
            y = both[:, (head - h) * LANES : (head - h + 1) * LANES]
            tri = tri_ref[head * 256 : (head + 1) * 256, :].reshape(32, 8, LANES)
            bias_h = jnp.broadcast_to(bias_ref[head * 8 : (head + 1) * 8, :][None], (32, 8, LANES))
            tail = jnp.stack([tri, bias_h], axis=1).reshape(512, LANES)
            out = jnp.where(lane < 96, y * factor, tail)
            send_ref[head * 512 : (head + 1) * 512, :] = out.astype(BF16)
    aux_ref[0:1, :] = flags2_ref[...].astype(F32)
    aux_ref[1:2, :] = chain_ref[...].astype(F32)
    aux_ref[2:3, :] = jnp.full((1, 256), offset_ref[row // 2], F32)


def in_hbm(*arrays):
    return [pltpu.with_memory_space_constraint(a, pltpu.HBM) for a in arrays]


def scratch_like(*arrays):
    return [(pltpu.SMEM if a.ndim == 1 else pltpu.VMEM)(a.shape, a.dtype) for a in arrays]


def pre(homolog, pair, flags, chain, offset, w_q, w_kv, w_bias, w_out, w_in):
    operands = (pair, w_out, w_in, flags, w_bias.T, homolog, w_q, w_kv, offset, flags.reshape(1, 256), chain.reshape(1, 256))
    return pl.pallas_call(
        pre_kernel,
        out_shape=(
            jax.ShapeDtypeStruct((4096, LANES), BF16),
            jax.ShapeDtypeStruct((512, 256), BF16),
            jax.ShapeDtypeStruct((256, LANES), BF16),
            jax.ShapeDtypeStruct((8, 256), F32),
        ),
        in_specs=[HBM] * 11,
        out_specs=(VMEM, VMEM, VMEM, VMEM),
        scratch_shapes=scratch_like(*operands)
        + [pltpu.VMEM((2048, LANES), F32), pltpu.VMEM((HEADS * 8, LANES), F32), pltpu.SemaphoreType.DMA((11,))],
        compiler_params=pltpu.CompilerParams(vmem_limit_bytes=32 * 2**20),
        name="pre",
    )(*in_hbm(*operands))


def mid_kernel(aux_ref, x_ref, out_ref, ps_ref, scores_ref):
    wide = (256, LANES)
    slot = lanes(wide) // 16

    def key_query(r):
        x = x_ref[r * 256 : (r + 1) * 256, :]
        return dot(x[:, DH : 2 * DH], x[:, :DH], NT)

    for r in range(N):
        scores_ref[r] = key_query(r)

    firsts, seconds = [], []
    for half in range(2):
        kept = [None, None]
        for c8 in range(8):
            starts = [(r * N + half * 8 + c8) * 16 for r in range(N)]
            part = jnp.concatenate([x_ref[s : s + 16, :] for s in starts], axis=0).astype(F32)
            part = turn(part, c8 * 16 - 96)
            old = kept[c8 % 2]
            pair_slots = (slot == c8) | (slot == (c8 + 1) % 8)
            kept[c8 % 2] = part if old is None else jnp.where(pair_slots, part, old)
        even = slot % 2 == 0
        firsts.append(jnp.where(even, kept[0], kept[1]))
        seconds.append(turn(jnp.where(even, kept[1], kept[0]), -16))
    first = jnp.concatenate(firsts, axis=1).reshape(N, 2, 8, 256)
    second = jnp.concatenate(seconds, axis=1).reshape(N, 2, 8, 256)
    bias = jnp.stack([first[:, 1], second[:, 1]], axis=1).reshape(256, 256)
    left = first[:, 0].reshape(LANES, 256).T.astype(BF16)
    right = second[:, 0].reshape(LANES, 256).astype(BF16)
    product = dot(left, right)
    high = product.astype(BF16).astype(F32)
    rest = product - high
    slot8 = lanes((LANES, LANES)) // 16

    for half in range(2):
        cols = slice(half * LANES, (half + 1) * LANES)
        high4 = high[:, cols].reshape(N, 2, 8, LANES)
        rest4 = rest[:, cols].reshape(N, 2, 8, LANES)
        upper = [(high4[:, u].reshape(LANES, LANES), turn(rest4[:, u].reshape(LANES, LANES), 16)) for u in range(2)]
        for parity in range(2):
            ours = slot8 % 2 == parity
            part_a = jnp.where(ours, *upper[0])
            part_b = turn(jnp.where(ours, *upper[1]), 64)
            near = (slot8 >= parity) & (slot8 < parity + 4)
            for merged, columns in (
                (jnp.where(near, part_a, part_b), (parity, parity + 2)),
                (jnp.where(near, part_b, part_a), (parity + 4, parity + 6)),
            ):
                for c8 in columns:
                    ps_ref[half * 8 + c8] = turn(merged, 32 - c8 * 16).reshape(N, 8, LANES)

    chain = jnp.broadcast_to(aux_ref[1:2, :], (LANES, 256))
    keep = jnp.broadcast_to(aux_ref[0:1, :], (LANES, 256))
    chain_t, keep_t = chain.T, keep.T
    bias_t = bias.T
    extra = []
    for half in range(2):
        cols = slice(half * LANES, (half + 1) * LANES)
        cross = jnp.where(chain_t != aux_ref[1:2, cols], aux_ref[2:3, cols], 0.0)
        extra.append(jnp.where(keep_t > 0.0, bias_t[:, cols] + cross, -1000000000.0))
    extra = jnp.concatenate(extra, axis=1)
    lane3 = lanes((N, 8, LANES))

    def finish(r, attended):
        both = jnp.concatenate([attended, attended, attended, attended], axis=0).T.reshape(N, 2, 8, LANES)
        chunk = jnp.where(lane3 < 64, both[:, 0], both[:, 1])
        chunk = jnp.where(lane3 % 64 < DH, chunk, ps_ref[:, r])
        out_ref[r * LANES : (r + 1) * LANES, :] = chunk.reshape(LANES, LANES).astype(BF16)

    def attend(r, exp_scores, total):
        return dot(x_ref[r * 256 : (r + 1) * 256, :], exp_scores, TN)[2 * DH : 3 * DH] / total

    coming = scores_ref[0]
    prev = None
    for r in range(N):
        scores = coming + extra
        if r + 1 < N:
            coming = scores_ref[r + 1]
        exp_scores = jnp.exp(scores - jnp.max(scores, axis=0, keepdims=True))
        total = jnp.sum(exp_scores, axis=0, keepdims=True)
        if prev is not None:
            finish(r - 1, attend(r - 1, *prev))
        prev = (exp_scores.astype(BF16), total)
    finish(N - 1, attend(N - 1, *prev))


def mid(received, aux):
    return pl.pallas_call(
        mid_kernel,
        out_shape=jax.ShapeDtypeStruct((2048, LANES), BF16),
        in_specs=[VMEM] * 2,
        out_specs=VMEM,
        scratch_shapes=[pltpu.VMEM((N, N, 8, LANES), F32), pltpu.VMEM((N, 256, 256), F32)],
        compiler_params=pltpu.CompilerParams(vmem_limit_bytes=32 * 2**20),
        name="mid",
    )(aux, received)


def post_kernel(x_ref, homolog_ref, pair_ref, msa_ref, pn_ref, wg_ref, wf_ref, wtg_ref, wtf_ref, out_ref, pair_out_ref, t_ref):
    x = x_ref[...].astype(F32).reshape(HEADS, 32, 8, LANES)
    group = lanes((32, 8, LANES)) // DH
    attended = []
    for g in range(2):
        parts = [None, None]
        for hh in range(4):
            for u in range(2):
                moved = turn(x[g * 4 + hh], hh * DH - u * 64)
                parts[u] = moved if hh == 0 else jnp.where(group == hh, moved, parts[u])
        attended.append(jnp.stack(parts, axis=1).reshape(512, LANES))
    attended = jnp.concatenate(attended, axis=1)
    gated = (jax.nn.sigmoid(dot(msa_ref[...], wg_ref[...])) * attended).astype(BF16)
    out = homolog_ref[...].reshape(512, 256).astype(F32) + dot(gated, wf_ref[...])
    out_ref[...] = out.astype(BF16).reshape(32, 16, 256)

    t = x.reshape(256, 8, LANES)
    t = t[:LANES] + t[LANES:]
    t_ref[...] = t.reshape(1024, LANES)
    upper, lower = [], []
    for i8 in range(8):
        rows = t_ref[pl.ds(i8, LANES, stride=8), :].T
        upper.append(rows[32:48] + rows[48:64])
        lower.append(rows[96:112] + rows[112:128])
    product_norm = standardize(jnp.concatenate(upper + lower, axis=0)).astype(BF16)
    update = jax.nn.sigmoid(dot(pn_ref[...], wtg_ref[...])) * dot(product_norm, wtf_ref[...])
    pair_out = pair_ref[...].reshape(N * N, LANES).astype(F32) + update
    pair_out_ref[...] = pair_out.astype(BF16).reshape(N, N, LANES)


def post(received, homolog, pair, msa_norm, pair_norm, w_gate, w_final, w_tri_gate, w_tri_final):
    return pl.pallas_call(
        post_kernel,
        out_shape=(jax.ShapeDtypeStruct(homolog.shape, BF16), jax.ShapeDtypeStruct(pair.shape, BF16)),
        in_specs=[VMEM] * 9,
        out_specs=(VMEM, VMEM),
        scratch_shapes=[pltpu.VMEM((1024, LANES), F32)],
        compiler_params=pltpu.CompilerParams(vmem_limit_bytes=32 * 2**20),
        name="post",
    )(received, homolog, pair, msa_norm, pair_norm, w_gate, w_final, w_tri_gate, w_tri_final)


def exchange(chunks):
    return lax.all_to_all(chunks, AXES, split_axis=0, concat_axis=0, tiled=True)


def local(
    homolog_tensor,
    pairwise_tensor,
    genuine_amino_flags,
    polymer_identity,
    asking_weights,
    attend_sigmoid_weights,
    lookup_content_weights,
    attend_final_weights,
    pairwise_logit_weights,
    crosspolymer_offset,
    outgoing_link_weights,
    incoming_link_weights,
    trimult_sigmoid_weights,
    trimult_final_weights,
):
    send, msa_norm, pair_norm, aux = pre(
        homolog_tensor,
        pairwise_tensor,
        genuine_amino_flags,
        polymer_identity,
        crosspolymer_offset,
        asking_weights,
        lookup_content_weights,
        pairwise_logit_weights,
        outgoing_link_weights,
        incoming_link_weights,
    )
    back = mid(exchange(send), aux)
    return post(
        exchange(back),
        homolog_tensor,
        pairwise_tensor,
        msa_norm,
        pair_norm,
        attend_sigmoid_weights,
        attend_final_weights,
        trimult_sigmoid_weights,
        trimult_final_weights,
    )


def solution(mesh):
    block = P("row", "col", None)
    in_specs = (block, block) + (P(),) * 12
    return jax.shard_map(local, mesh=mesh, in_specs=in_specs, out_specs=(block, block), check_vma=False)
```

```python
import jax
import jax.numpy as jnp
from jax import lax
from jax.experimental import pallas as pl
from jax.experimental.pallas import tpu as pltpu
from jax.sharding import PartitionSpec as P

AXES = ("row", "col")
F32 = jnp.float32
BF16 = jnp.bfloat16
N = 16
HEADS = 8
DH = 32
LANES = 128
VMEM = pl.BlockSpec(memory_space=pltpu.VMEM)
HBM = pl.BlockSpec(memory_space=pltpu.HBM)
NT = (((1,), (1,)), ((), ()))
TN = (((0,), (0,)), ((), ()))


def standardize(tensor):
    tensor = tensor.astype(F32)
    center = tensor - jnp.mean(tensor, axis=-1, keepdims=True)
    spread = jnp.mean(center * center, axis=-1, keepdims=True)
    return center * lax.rsqrt(spread + 1e-05)


def dot(a, b, dims=(((1,), (0,)), ((), ()))):
    return lax.dot_general(a, b, dims, preferred_element_type=F32)


def lanes(shape):
    return lax.broadcasted_iota(jnp.int32, shape, len(shape) - 1)


def turn(x, by):
    by = by % LANES
    return x if by == 0 else pltpu.roll(x, by, x.ndim - 1)


def fetch(pairs, sems):
    copies = [pltpu.make_async_copy(source, target, sems.at[i]) for i, (source, target) in enumerate(pairs)]
    for copy in copies:
        copy.start()
    return copies


def pre_kernel(
    pair_hbm, wo_hbm, wi_hbm, flags_hbm, wb_hbm, x_hbm, wq_hbm, wkv_hbm, offset_hbm, flags2_hbm, chain_hbm,
    send_ref, msa_ref, pn_ref, aux_ref,
    pair_ref, wo_ref, wi_ref, flags_ref, wb_ref, x_ref, wq_ref, wkv_ref, offset_ref, flags2_ref, chain_ref, tri_ref, bias_ref, sems,
):
    row, col = lax.axis_index("row"), lax.axis_index("col")
    copies = fetch(
        (
            (x_hbm, x_ref),
            (pair_hbm, pair_ref),
            (wo_hbm, wo_ref),
            (wi_hbm, wi_ref),
            (flags_hbm, flags_ref),
            (wb_hbm, wb_ref),
            (wq_hbm, wq_ref),
            (wkv_hbm, wkv_ref),
            (offset_hbm, offset_ref),
            (flags2_hbm, flags2_ref),
            (chain_hbm, chain_ref),
        ),
        sems,
    )
    copies[0].wait()
    msa_norm = standardize(x_ref[...].reshape(512, 256)).astype(BF16)
    msa_ref[...] = msa_norm
    for copy in copies[1:]:
        copy.wait()
    pair_norm = standardize(pair_ref[...].reshape(N * N, LANES)).astype(BF16)
    pn_ref[...] = pair_norm
    lane8 = lanes((LANES, LANES))
    sides = []
    for w_ref in (wo_ref, wi_ref):
        projected = dot(pair_norm, w_ref[...])
        sides.append((jax.nn.sigmoid(projected[:, :LANES]) * projected[:, LANES:]).T)
    for k in range(N):
        half, k8 = k // 8, k % 8
        flag = flags_ref[row * N + k].astype(F32)
        left, right = (side[:, half * LANES : (half + 1) * LANES] for side in sides)
        part = jnp.where(lane8 < 112, turn(left, 96 - k8 * 16), turn(right, 112 - k8 * 16)) * flag
        tri_ref[pl.ds(half * 1024 + k8, LANES, stride=8), :] = part
    bias = dot(wb_ref[...], pair_norm, NT)
    for i in range(8):
        part = jnp.where(lane8[:8] < 112, turn(bias[:, :LANES], 96 - i * 16), turn(bias[:, LANES:], 112 - i * 16))
        bias_ref[pl.ds(i, HEADS, stride=8), :] = part

    lane = lanes((512, LANES))
    tile_row = lax.broadcasted_iota(jnp.int32, (N, LANES), 0)
    keep = jnp.ones((N, LANES), F32)
    for res in range(N):
        keep = jnp.where(tile_row == res, flags_ref[col * N + res].astype(F32), keep)
    tile_lane = lanes((N, LANES))
    factor = jnp.where(tile_lane < DH, DH**-0.5, jnp.where(tile_lane < 2 * DH, keep, 1.0))
    factor = jnp.broadcast_to(factor[None], (32, N, LANES)).reshape(512, LANES)
    for h in range(0, HEADS, 2):
        parts = []
        for head in (h, h + 1):
            cut = slice(head * DH, (head + 1) * DH)
            cut_v = slice(256 + head * DH, 256 + (head + 1) * DH)
            parts += [wq_ref[:, cut], wkv_ref[:, cut], wkv_ref[:, cut_v], wq_ref[:, cut]]
        both = dot(msa_norm, jnp.concatenate(parts, axis=1))
        for head in (h, h + 1):
            y = both[:, (head - h) * LANES : (head - h + 1) * LANES]
            tri = tri_ref[head * 256 : (head + 1) * 256, :].reshape(32, 8, LANES)
            bias_h = jnp.broadcast_to(bias_ref[head * 8 : (head + 1) * 8, :][None], (32, 8, LANES))
            tail = jnp.stack([tri, bias_h], axis=1).reshape(512, LANES)
            out = jnp.where(lane < 96, y * factor, tail)
            send_ref[head * 512 : (head + 1) * 512, :] = out.astype(BF16)
    aux_ref[0:1, :] = flags2_ref[...].astype(F32)
    aux_ref[1:2, :] = chain_ref[...].astype(F32)
    aux_ref[2:3, :] = jnp.full((1, 256), offset_ref[row // 2], F32)


def in_hbm(*arrays):
    return [pltpu.with_memory_space_constraint(a, pltpu.HBM) for a in arrays]


def scratch_like(*arrays):
    return [(pltpu.SMEM if a.ndim == 1 else pltpu.VMEM)(a.shape, a.dtype) for a in arrays]


def pre(homolog, pair, flags, chain, offset, w_q, w_kv, w_bias, w_out, w_in):
    operands = (pair, w_out, w_in, flags, w_bias.T, homolog, w_q, w_kv, offset, flags.reshape(1, 256), chain.reshape(1, 256))
    return pl.pallas_call(
        pre_kernel,
        out_shape=(
            jax.ShapeDtypeStruct((4096, LANES), BF16),
            jax.ShapeDtypeStruct((512, 256), BF16),
            jax.ShapeDtypeStruct((256, LANES), BF16),
            jax.ShapeDtypeStruct((8, 256), F32),
        ),
        in_specs=[HBM] * 11,
        out_specs=(VMEM, VMEM, VMEM, VMEM),
        scratch_shapes=scratch_like(*operands)
        + [pltpu.VMEM((2048, LANES), F32), pltpu.VMEM((HEADS * 8, LANES), F32), pltpu.SemaphoreType.DMA((11,))],
        compiler_params=pltpu.CompilerParams(vmem_limit_bytes=32 * 2**20),
        name="pre",
    )(*in_hbm(*operands))


def mid_kernel(aux_ref, x_ref, out_ref, ps_ref, scores_ref):
    wide = (256, LANES)
    slot = lanes(wide) // 16

    def key_query(r):
        x = x_ref[r * 256 : (r + 1) * 256, :]
        return dot(x[:, DH : 2 * DH], x[:, :DH], NT)

    for r in range(N):
        scores_ref[r] = key_query(r)

    firsts, seconds = [], []
    for half in range(2):
        kept = [None, None]
        for c8 in range(8):
            starts = [(r * N + half * 8 + c8) * 16 for r in range(N)]
            part = jnp.concatenate([x_ref[s : s + 16, :] for s in starts], axis=0).astype(F32)
            part = turn(part, c8 * 16 - 96)
            old = kept[c8 % 2]
            pair_slots = (slot == c8) | (slot == (c8 + 1) % 8)
            kept[c8 % 2] = part if old is None else jnp.where(pair_slots, part, old)
        even = slot % 2 == 0
        firsts.append(jnp.where(even, kept[0], kept[1]))
        seconds.append(turn(jnp.where(even, kept[1], kept[0]), -16))
    first = jnp.concatenate(firsts, axis=1).reshape(N, 2, 8, 256)
    second = jnp.concatenate(seconds, axis=1).reshape(N, 2, 8, 256)
    bias = jnp.stack([first[:, 1], second[:, 1]], axis=1).reshape(256, 256)
    left = first[:, 0].reshape(LANES, 256).T.astype(BF16)
    right = second[:, 0].reshape(LANES, 256).astype(BF16)
    product = dot(left, right)
    high = product.astype(BF16).astype(F32)
    rest = product - high
    slot8 = lanes((LANES, LANES)) // 16

    for half in range(2):
        cols = slice(half * LANES, (half + 1) * LANES)
        high4 = high[:, cols].reshape(N, 2, 8, LANES)
        rest4 = rest[:, cols].reshape(N, 2, 8, LANES)
        upper = [(high4[:, u].reshape(LANES, LANES), turn(rest4[:, u].reshape(LANES, LANES), 16)) for u in range(2)]
        for parity in range(2):
            ours = slot8 % 2 == parity
            part_a = jnp.where(ours, *upper[0])
            part_b = turn(jnp.where(ours, *upper[1]), 64)
            near = (slot8 >= parity) & (slot8 < parity + 4)
            for merged, columns in (
                (jnp.where(near, part_a, part_b), (parity, parity + 2)),
                (jnp.where(near, part_b, part_a), (parity + 4, parity + 6)),
            ):
                for c8 in columns:
                    ps_ref[half * 8 + c8] = turn(merged, 32 - c8 * 16).reshape(N, 8, LANES)

    chain = jnp.broadcast_to(aux_ref[1:2, :], (LANES, 256))
    keep = jnp.broadcast_to(aux_ref[0:1, :], (LANES, 256))
    chain_t, keep_t = chain.T, keep.T
    bias_t = bias.T
    extra = []
    for half in range(2):
        cols = slice(half * LANES, (half + 1) * LANES)
        cross = jnp.where(chain_t != aux_ref[1:2, cols], aux_ref[2:3, cols], 0.0)
        extra.append(jnp.where(keep_t > 0.0, bias_t[:, cols] + cross, -1000000000.0))
    extra = jnp.concatenate(extra, axis=1)
    lane3 = lanes((N, 8, LANES))

    def finish(r, attended):
        both = jnp.concatenate([attended, attended, attended, attended], axis=0).T.reshape(N, 2, 8, LANES)
        chunk = jnp.where(lane3 < 64, both[:, 0], both[:, 1])
        chunk = jnp.where(lane3 % 64 < DH, chunk, ps_ref[:, r])
        out_ref[r * LANES : (r + 1) * LANES, :] = chunk.reshape(LANES, LANES).astype(BF16)

    def attend(r, exp_scores, total):
        return dot(x_ref[r * 256 : (r + 1) * 256, :], exp_scores, TN)[2 * DH : 3 * DH] / total

    coming = scores_ref[0]
    prev = None
    done = []
    for r in range(N):
        scores = coming + extra
        if r + 1 < N:
            coming = scores_ref[r + 1]
        exp_scores = jnp.exp(scores - jnp.max(scores, axis=0, keepdims=True))
        total = jnp.sum(exp_scores, axis=0, keepdims=True)
        if prev is not None:
            done.append(attend(r - 1, *prev))
        prev = (exp_scores.astype(BF16), total)
    done.append(attend(N - 1, *prev))
    for r in range(N):
        finish(r, done[r])


def mid(received, aux):
    return pl.pallas_call(
        mid_kernel,
        out_shape=jax.ShapeDtypeStruct((2048, LANES), BF16),
        in_specs=[VMEM] * 2,
        out_specs=VMEM,
        scratch_shapes=[pltpu.VMEM((N, N, 8, LANES), F32), pltpu.VMEM((N, 256, 256), F32)],
        compiler_params=pltpu.CompilerParams(vmem_limit_bytes=32 * 2**20),
        name="mid",
    )(aux, received)


def post_kernel(x_ref, homolog_ref, pair_ref, msa_ref, pn_ref, wg_ref, wf_ref, wtg_ref, wtf_ref, out_ref, pair_out_ref, t_ref):
    x = x_ref[...].astype(F32).reshape(HEADS, 32, 8, LANES)
    group = lanes((32, 8, LANES)) // DH
    attended = []
    for g in range(2):
        parts = [None, None]
        for hh in range(4):
            for u in range(2):
                moved = turn(x[g * 4 + hh], hh * DH - u * 64)
                parts[u] = moved if hh == 0 else jnp.where(group == hh, moved, parts[u])
        attended.append(jnp.stack(parts, axis=1).reshape(512, LANES))
    attended = jnp.concatenate(attended, axis=1)
    gated = (jax.nn.sigmoid(dot(msa_ref[...], wg_ref[...])) * attended).astype(BF16)
    out = homolog_ref[...].reshape(512, 256).astype(F32) + dot(gated, wf_ref[...])
    out_ref[...] = out.astype(BF16).reshape(32, 16, 256)

    t = x.reshape(256, 8, LANES)
    t = t[:LANES] + t[LANES:]
    t_ref[...] = t.reshape(1024, LANES)
    upper, lower = [], []
    for i8 in range(8):
        rows = t_ref[pl.ds(i8, LANES, stride=8), :].T
        upper.append(rows[32:48] + rows[48:64])
        lower.append(rows[96:112] + rows[112:128])
    product_norm = standardize(jnp.concatenate(upper + lower, axis=0)).astype(BF16)
    update = jax.nn.sigmoid(dot(pn_ref[...], wtg_ref[...])) * dot(product_norm, wtf_ref[...])
    pair_out = pair_ref[...].reshape(N * N, LANES).astype(F32) + update
    pair_out_ref[...] = pair_out.astype(BF16).reshape(N, N, LANES)


def post(received, homolog, pair, msa_norm, pair_norm, w_gate, w_final, w_tri_gate, w_tri_final):
    return pl.pallas_call(
        post_kernel,
        out_shape=(jax.ShapeDtypeStruct(homolog.shape, BF16), jax.ShapeDtypeStruct(pair.shape, BF16)),
        in_specs=[VMEM] * 9,
        out_specs=(VMEM, VMEM),
        scratch_shapes=[pltpu.VMEM((1024, LANES), F32)],
        compiler_params=pltpu.CompilerParams(vmem_limit_bytes=32 * 2**20),
        name="post",
    )(received, homolog, pair, msa_norm, pair_norm, w_gate, w_final, w_tri_gate, w_tri_final)


def exchange(chunks):
    return lax.all_to_all(chunks, AXES, split_axis=0, concat_axis=0, tiled=True)


def local(
    homolog_tensor,
    pairwise_tensor,
    genuine_amino_flags,
    polymer_identity,
    asking_weights,
    attend_sigmoid_weights,
    lookup_content_weights,
    attend_final_weights,
    pairwise_logit_weights,
    crosspolymer_offset,
    outgoing_link_weights,
    incoming_link_weights,
    trimult_sigmoid_weights,
    trimult_final_weights,
):
    send, msa_norm, pair_norm, aux = pre(
        homolog_tensor,
        pairwise_tensor,
        genuine_amino_flags,
        polymer_identity,
        crosspolymer_offset,
        asking_weights,
        lookup_content_weights,
        pairwise_logit_weights,
        outgoing_link_weights,
        incoming_link_weights,
    )
    back = mid(exchange(send), aux)
    return post(
        exchange(back),
        homolog_tensor,
        pairwise_tensor,
        msa_norm,
        pair_norm,
        attend_sigmoid_weights,
        attend_final_weights,
        trimult_sigmoid_weights,
        trimult_final_weights,
    )


def solution(mesh):
    block = P("row", "col", None)
    in_specs = (block, block) + (P(),) * 12
    return jax.shard_map(local, mesh=mesh, in_specs=in_specs, out_specs=(block, block), check_vma=False)
```

```python
import jax
import jax.numpy as jnp
from jax import lax
from jax.experimental import pallas as pl
from jax.experimental.pallas import tpu as pltpu
from jax.sharding import PartitionSpec as P

AXES = ("row", "col")
F32 = jnp.float32
BF16 = jnp.bfloat16
N = 16
HEADS = 8
DH = 32
LANES = 128
VMEM = pl.BlockSpec(memory_space=pltpu.VMEM)
HBM = pl.BlockSpec(memory_space=pltpu.HBM)
NT = (((1,), (1,)), ((), ()))
TN = (((0,), (0,)), ((), ()))


def standardize(tensor):
    tensor = tensor.astype(F32)
    center = tensor - jnp.mean(tensor, axis=-1, keepdims=True)
    spread = jnp.mean(center * center, axis=-1, keepdims=True)
    return center * lax.rsqrt(spread + 1e-05)


def dot(a, b, dims=(((1,), (0,)), ((), ()))):
    return lax.dot_general(a, b, dims, preferred_element_type=F32)


def lanes(shape):
    return lax.broadcasted_iota(jnp.int32, shape, len(shape) - 1)


def turn(x, by):
    by = by % LANES
    return x if by == 0 else pltpu.roll(x, by, x.ndim - 1)


def fetch(pairs, sems):
    copies = [pltpu.make_async_copy(source, target, sems.at[i]) for i, (source, target) in enumerate(pairs)]
    for copy in copies:
        copy.start()
    return copies


def pre_kernel(
    pair_hbm, wo_hbm, wi_hbm, flags_hbm, wb_hbm, x_hbm, wq_hbm, wkv_hbm, offset_hbm, flags2_hbm, chain_hbm,
    send_ref, msa_ref, pn_ref, aux_ref,
    pair_ref, wo_ref, wi_ref, flags_ref, wb_ref, x_ref, wq_ref, wkv_ref, offset_ref, flags2_ref, chain_ref, tri_ref, bias_ref, sems,
):
    row, col = lax.axis_index("row"), lax.axis_index("col")
    copies = fetch(
        (
            (x_hbm, x_ref),
            (pair_hbm, pair_ref),
            (wo_hbm, wo_ref),
            (wi_hbm, wi_ref),
            (flags_hbm, flags_ref),
            (wb_hbm, wb_ref),
            (wq_hbm, wq_ref),
            (wkv_hbm, wkv_ref),
            (offset_hbm, offset_ref),
            (flags2_hbm, flags2_ref),
            (chain_hbm, chain_ref),
        ),
        sems,
    )
    copies[0].wait()
    msa_norm = standardize(x_ref[...].reshape(512, 256)).astype(BF16)
    msa_ref[...] = msa_norm
    for copy in copies[1:]:
        copy.wait()
    pair_norm = standardize(pair_ref[...].reshape(N * N, LANES)).astype(BF16)
    pn_ref[...] = pair_norm
    lane8 = lanes((LANES, LANES))
    sides = []
    for w_ref in (wo_ref, wi_ref):
        projected = dot(pair_norm, w_ref[...])
        sides.append((jax.nn.sigmoid(projected[:, :LANES]) * projected[:, LANES:]).T)
    for k in range(N):
        half, k8 = k // 8, k % 8
        flag = flags_ref[row * N + k].astype(F32)
        left, right = (side[:, half * LANES : (half + 1) * LANES] for side in sides)
        part = jnp.where(lane8 < 112, turn(left, 96 - k8 * 16), turn(right, 112 - k8 * 16)) * flag
        tri_ref[pl.ds(half * 1024 + k8, LANES, stride=8), :] = part
    bias = dot(wb_ref[...], pair_norm, NT)
    for i in range(8):
        part = jnp.where(lane8[:8] < 112, turn(bias[:, :LANES], 96 - i * 16), turn(bias[:, LANES:], 112 - i * 16))
        bias_ref[pl.ds(i, HEADS, stride=8), :] = part

    lane = lanes((512, LANES))
    tile_row = lax.broadcasted_iota(jnp.int32, (N, LANES), 0)
    keep = jnp.ones((N, LANES), F32)
    for res in range(N):
        keep = jnp.where(tile_row == res, flags_ref[col * N + res].astype(F32), keep)
    tile_lane = lanes((N, LANES))
    factor = jnp.where(tile_lane < DH, DH**-0.5, jnp.where(tile_lane < 2 * DH, keep, 1.0))
    factor = jnp.broadcast_to(factor[None], (32, N, LANES)).reshape(512, LANES)
    for h in range(0, HEADS, 2):
        parts = []
        for head in (h, h + 1):
            cut = slice(head * DH, (head + 1) * DH)
            cut_v = slice(256 + head * DH, 256 + (head + 1) * DH)
            parts += [wq_ref[:, cut], wkv_ref[:, cut], wkv_ref[:, cut_v], wq_ref[:, cut]]
        both = dot(msa_norm, jnp.concatenate(parts, axis=1))
        for head in (h, h + 1):
            y = both[:, (head - h) * LANES : (head - h + 1) * LANES]
            tri = tri_ref[head * 256 : (head + 1) * 256, :].reshape(32, 8, LANES)
            bias_h = jnp.broadcast_to(bias_ref[head * 8 : (head + 1) * 8, :][None], (32, 8, LANES))
            tail = jnp.stack([tri, bias_h], axis=1).reshape(512, LANES)
            out = jnp.where(lane < 96, y * factor, tail)
            send_ref[head * 512 : (head + 1) * 512, :] = out.astype(BF16)
    aux_ref[0:1, :] = flags2_ref[...].astype(F32)
    aux_ref[1:2, :] = chain_ref[...].astype(F32)
    aux_ref[2:3, :] = jnp.full((1, 256), offset_ref[row // 2], F32)


def in_hbm(*arrays):
    return [pltpu.with_memory_space_constraint(a, pltpu.HBM) for a in arrays]


def scratch_like(*arrays):
    return [(pltpu.SMEM if a.ndim == 1 else pltpu.VMEM)(a.shape, a.dtype) for a in arrays]


def pre(homolog, pair, flags, chain, offset, w_q, w_kv, w_bias, w_out, w_in):
    operands = (pair, w_out, w_in, flags, w_bias.T, homolog, w_q, w_kv, offset, flags.reshape(1, 256), chain.reshape(1, 256))
    return pl.pallas_call(
        pre_kernel,
        out_shape=(
            jax.ShapeDtypeStruct((4096, LANES), BF16),
            jax.ShapeDtypeStruct((512, 256), BF16),
            jax.ShapeDtypeStruct((256, LANES), BF16),
            jax.ShapeDtypeStruct((8, 256), F32),
        ),
        in_specs=[HBM] * 11,
        out_specs=(VMEM, VMEM, VMEM, VMEM),
        scratch_shapes=scratch_like(*operands)
        + [pltpu.VMEM((2048, LANES), F32), pltpu.VMEM((HEADS * 8, LANES), F32), pltpu.SemaphoreType.DMA((11,))],
        compiler_params=pltpu.CompilerParams(vmem_limit_bytes=32 * 2**20),
        name="pre",
    )(*in_hbm(*operands))


def mid_kernel(aux_ref, x_ref, out_ref, ps_ref, scores_ref):
    wide = (256, LANES)
    slot = lanes(wide) // 16

    def key_query(r):
        x = x_ref[r * 256 : (r + 1) * 256, :]
        return dot(x[:, DH : 2 * DH], x[:, :DH], NT)

    for r in range(N):
        scores_ref[r] = key_query(r)

    firsts, seconds = [], []
    for half in range(2):
        kept = [None, None]
        for c8 in range(8):
            starts = [(r * N + half * 8 + c8) * 16 for r in range(N)]
            part = jnp.concatenate([x_ref[s : s + 16, :] for s in starts], axis=0).astype(F32)
            part = turn(part, c8 * 16 - 96)
            old = kept[c8 % 2]
            pair_slots = (slot == c8) | (slot == (c8 + 1) % 8)
            kept[c8 % 2] = part if old is None else jnp.where(pair_slots, part, old)
        even = slot % 2 == 0
        firsts.append(jnp.where(even, kept[0], kept[1]))
        seconds.append(turn(jnp.where(even, kept[1], kept[0]), -16))
    first = jnp.concatenate(firsts, axis=1).reshape(N, 2, 8, 256)
    second = jnp.concatenate(seconds, axis=1).reshape(N, 2, 8, 256)
    bias = jnp.stack([first[:, 1], second[:, 1]], axis=1).reshape(256, 256)
    left = first[:, 0].reshape(LANES, 256).T.astype(BF16)
    right = second[:, 0].reshape(LANES, 256).astype(BF16)
    product = dot(left, right)
    high = product.astype(BF16).astype(F32)
    rest = product - high
    slot8 = lanes((LANES, LANES)) // 16

    for half in range(2):
        cols = slice(half * LANES, (half + 1) * LANES)
        high4 = high[:, cols].reshape(N, 2, 8, LANES)
        rest4 = rest[:, cols].reshape(N, 2, 8, LANES)
        upper = [(high4[:, u].reshape(LANES, LANES), turn(rest4[:, u].reshape(LANES, LANES), 16)) for u in range(2)]
        for parity in range(2):
            ours = slot8 % 2 == parity
            part_a = jnp.where(ours, *upper[0])
            part_b = turn(jnp.where(ours, *upper[1]), 64)
            near = (slot8 >= parity) & (slot8 < parity + 4)
            for merged, columns in (
                (jnp.where(near, part_a, part_b), (parity, parity + 2)),
                (jnp.where(near, part_b, part_a), (parity + 4, parity + 6)),
            ):
                for c8 in columns:
                    ps_ref[half * 8 + c8] = turn(merged, 32 - c8 * 16).reshape(N, 8, LANES)

    chain = jnp.broadcast_to(aux_ref[1:2, :], (LANES, 256))
    keep = jnp.broadcast_to(aux_ref[0:1, :], (LANES, 256))
    chain_t, keep_t = chain.T, keep.T
    bias_t = bias.T
    extra = []
    for half in range(2):
        cols = slice(half * LANES, (half + 1) * LANES)
        cross = jnp.where(chain_t != aux_ref[1:2, cols], aux_ref[2:3, cols], 0.0)
        extra.append(jnp.where(keep_t > 0.0, bias_t[:, cols] + cross, -1000000000.0))
    extra = jnp.concatenate(extra, axis=1)
    lane3 = lanes((N, 8, LANES))

    def finish(r, attended):
        attended = attended.astype(BF16)
        both = jnp.concatenate([attended, attended, attended, attended], axis=0).T.astype(F32).reshape(N, 2, 8, LANES)
        chunk = jnp.where(lane3 < 64, both[:, 0], both[:, 1])
        chunk = jnp.where(lane3 % 64 < DH, chunk, ps_ref[:, r])
        out_ref[r * LANES : (r + 1) * LANES, :] = chunk.reshape(LANES, LANES).astype(BF16)

    def attend(r, exp_scores, total):
        return dot(x_ref[r * 256 : (r + 1) * 256, :], exp_scores, TN)[2 * DH : 3 * DH] / total

    coming = scores_ref[0]
    prev = None
    done = []
    for r in range(N):
        scores = coming + extra
        if r + 1 < N:
            coming = scores_ref[r + 1]
        exp_scores = jnp.exp(scores - jnp.max(scores, axis=0, keepdims=True))
        total = jnp.sum(exp_scores, axis=0, keepdims=True)
        if prev is not None:
            done.append(attend(r - 1, *prev))
        prev = (exp_scores.astype(BF16), total)
    done.append(attend(N - 1, *prev))
    for r in range(N):
        finish(r, done[r])


def mid(received, aux):
    return pl.pallas_call(
        mid_kernel,
        out_shape=jax.ShapeDtypeStruct((2048, LANES), BF16),
        in_specs=[VMEM] * 2,
        out_specs=VMEM,
        scratch_shapes=[pltpu.VMEM((N, N, 8, LANES), F32), pltpu.VMEM((N, 256, 256), F32)],
        compiler_params=pltpu.CompilerParams(vmem_limit_bytes=32 * 2**20),
        name="mid",
    )(aux, received)


def post_kernel(x_ref, homolog_ref, pair_ref, msa_ref, pn_ref, wg_ref, wf_ref, wtg_ref, wtf_ref, out_ref, pair_out_ref, t_ref):
    x = x_ref[...].astype(F32).reshape(HEADS, 32, 8, LANES)
    group = lanes((32, 8, LANES)) // DH
    attended = []
    for g in range(2):
        parts = [None, None]
        for hh in range(4):
            for u in range(2):
                moved = turn(x[g * 4 + hh], hh * DH - u * 64)
                parts[u] = moved if hh == 0 else jnp.where(group == hh, moved, parts[u])
        attended.append(jnp.stack(parts, axis=1).reshape(512, LANES))
    attended = jnp.concatenate(attended, axis=1)
    gated = (jax.nn.sigmoid(dot(msa_ref[...], wg_ref[...])) * attended).astype(BF16)
    out = homolog_ref[...].reshape(512, 256).astype(F32) + dot(gated, wf_ref[...])
    out_ref[...] = out.astype(BF16).reshape(32, 16, 256)

    t = x.reshape(256, 8, LANES)
    t = t[:LANES] + t[LANES:]
    t_ref[...] = t.reshape(1024, LANES)
    upper, lower = [], []
    for i8 in range(8):
        rows = t_ref[pl.ds(i8, LANES, stride=8), :].T
        upper.append(rows[32:48] + rows[48:64])
        lower.append(rows[96:112] + rows[112:128])
    product_norm = standardize(jnp.concatenate(upper + lower, axis=0)).astype(BF16)
    update = jax.nn.sigmoid(dot(pn_ref[...], wtg_ref[...])) * dot(product_norm, wtf_ref[...])
    pair_out = pair_ref[...].reshape(N * N, LANES).astype(F32) + update
    pair_out_ref[...] = pair_out.astype(BF16).reshape(N, N, LANES)


def post(received, homolog, pair, msa_norm, pair_norm, w_gate, w_final, w_tri_gate, w_tri_final):
    return pl.pallas_call(
        post_kernel,
        out_shape=(jax.ShapeDtypeStruct(homolog.shape, BF16), jax.ShapeDtypeStruct(pair.shape, BF16)),
        in_specs=[VMEM] * 9,
        out_specs=(VMEM, VMEM),
        scratch_shapes=[pltpu.VMEM((1024, LANES), F32)],
        compiler_params=pltpu.CompilerParams(vmem_limit_bytes=32 * 2**20),
        name="post",
    )(received, homolog, pair, msa_norm, pair_norm, w_gate, w_final, w_tri_gate, w_tri_final)


def exchange(chunks):
    return lax.all_to_all(chunks, AXES, split_axis=0, concat_axis=0, tiled=True)


def local(
    homolog_tensor,
    pairwise_tensor,
    genuine_amino_flags,
    polymer_identity,
    asking_weights,
    attend_sigmoid_weights,
    lookup_content_weights,
    attend_final_weights,
    pairwise_logit_weights,
    crosspolymer_offset,
    outgoing_link_weights,
    incoming_link_weights,
    trimult_sigmoid_weights,
    trimult_final_weights,
):
    send, msa_norm, pair_norm, aux = pre(
        homolog_tensor,
        pairwise_tensor,
        genuine_amino_flags,
        polymer_identity,
        crosspolymer_offset,
        asking_weights,
        lookup_content_weights,
        pairwise_logit_weights,
        outgoing_link_weights,
        incoming_link_weights,
    )
    back = mid(exchange(send), aux)
    return post(
        exchange(back),
        homolog_tensor,
        pairwise_tensor,
        msa_norm,
        pair_norm,
        attend_sigmoid_weights,
        attend_final_weights,
        trimult_sigmoid_weights,
        trimult_final_weights,
    )


def solution(mesh):
    block = P("row", "col", None)
    in_specs = (block, block) + (P(),) * 12
    return jax.shard_map(local, mesh=mesh, in_specs=in_specs, out_specs=(block, block), check_vma=False)
```
